32 devices in a mesh: gx: 8 (over z, core), gy: 4 (over y, x).
Axes of the slice: x: 2, y: 2, z: 4, core: 2. Of those that a mesh axis runs over, the one named last changes fastest.
Arguments:
- u_velocity: float32 [128, 128, 512], P('gx', 'gy'), may hold values from -5 to 5
- v_velocity: float32 [128, 128, 512], P('gx', 'gy'), may hold values from -5 to 5
- w_velocity: float32 [128, 128, 512], P('gx', 'gy'), may hold values from -5 to 5
- viscosity: float32 [128, 128, 512], P('gx', 'gy'), may hold values from 0.5 to 2
- cell_width: float32 [128], P('gx'), may hold values from 0.003 to 0.008
Outputs:
- u_next: float32 [128, 128, 512], P('gx', 'gy')
- v_next: float32 [128, 128, 512], P('gx', 'gy')
- w_next: float32 [128, 128, 512], P('gx', 'gy')
The draws below stay inside these ranges and needn't reach their ends.
All inputs are finite; a program needn't handle non-finite values.
Results may differ from the reference program's by a relative error of at most 0.0002.
Values sent between devices are 32-bit elements; how exact they have to be, the bound alone decides.
A program may use at most 128 MiB of HBM per device.

```python
import math
import jax
import jax.numpy as jnp
from jax import lax

CZ = 512
NX = 128
NY = 128


def velocity_draw(key, salt):
    key = jax.random.fold_in(key, salt)
    first_key = jax.random.fold_in(key, 0)
    return jnp.clip(jax.random.normal(first_key, (NX, NY, CZ), jnp.float32), -5.0, 5.0)


def draw_u_velocity(key, part):
    return velocity_draw(key, 11)


def draw_v_velocity(key, part):
    return velocity_draw(key, 23)


def draw_w_velocity(key, part):
    return velocity_draw(key, 37)


def shard_levels(own_key, dims, cuts, least, largest):
    gain = 1.0
    for dim, parts in cuts:
        draws = jax.random.uniform(jax.random.fold_in(jax.random.fold_in(own_key, 6), dim), (parts,), jnp.float32, least / len(cuts), largest / len(cuts))
        gain = gain * jnp.repeat(jnp.exp(draws), dims[dim] // parts).reshape((-1,) + (1,) * (len(dims) - 1 - dim))
    return gain


def setup_inputs(seed: int = 0) -> dict:
    splits = jax.random.split(jax.random.key(seed), 6)
    return {
        "u_velocity": draw_u_velocity(jax.random.fold_in(splits[5], 71), 0),
        "v_velocity": draw_v_velocity(jax.random.fold_in(splits[5], 71), 0),
        "w_velocity": draw_w_velocity(jax.random.fold_in(splits[5], 71), 0),
        "viscosity": jnp.clip(jnp.exp(math.log(2.0) - 1.3862944 * jax.random.uniform(splits[3], (NX, NY, CZ), jnp.float32) ** shard_levels(splits[3], (NX, NY, CZ), ((0, 8), (1, 4)), -0.2, 0.2)), 0.5, 2.0),
        "cell_width": jnp.clip(jnp.exp(math.log(0.008) - 0.9808293 * jax.random.uniform(splits[4], (NX,), jnp.float32) ** shard_levels(splits[4], (NX,), ((0, 8),), -0.2, 0.2)), 0.003, 0.008),
    }


time_step = 0.0125
lateral_step = 0.5
vertical_step = 0.5


def thomas(sub_coef, diag_coef, sup_coef, right_side):
    def forward(state_pair, row_data):
        ratio_prev, value_prev = state_pair
        sub_row, diag_row, sup_row, side_row = row_data
        denom = diag_row - sub_row * ratio_prev
        ratio_now = sup_row / denom
        value_now = (side_row - sub_row[None] * value_prev) / denom[None]
        return (ratio_now, value_now), (ratio_now, value_now)

    start = (jnp.zeros_like(diag_coef[0]), jnp.zeros_like(right_side[0]))
    _, (ratios, values) = lax.scan(forward, start, (sub_coef, diag_coef, sup_coef, right_side))

    def backward(after, row_data):
        ratio_row, value_row = row_data
        result = value_row - ratio_row[None] * after
        return result, result

    _, solved = lax.scan(backward, jnp.zeros_like(right_side[0]), (ratios, values), reverse=True)
    return solved


def explicit_terms(padded, widths):
    u_all, v_all, w_all, viscous = padded[0], padded[1], padded[2], padded[3]
    rows_x = padded.shape[1] - 2
    rows_y = padded.shape[2] - 2
    rows_z = padded.shape[3] - 2

    def interior(values_in, shift_x, shift_y, shift_z):
        return values_in[1 + shift_x:1 + shift_x + rows_x, 1 + shift_y:1 + shift_y + rows_y, 1 + shift_z:1 + shift_z + rows_z]

    width_mid = widths[1:-1][:, None, None]
    width_low = widths[:-2][:, None, None]
    width_high = widths[2:][:, None, None]
    centre_span = 0.5 * width_low + width_mid + 0.5 * width_high
    visc_mid = interior(viscous, 0, 0, 0)
    below_coef = time_step * 0.5 * (visc_mid + interior(viscous, -1, 0, 0)) / (width_mid * 0.5 * (width_low + width_mid))
    above_coef = time_step * 0.5 * (visc_mid + interior(viscous, 1, 0, 0)) / (width_mid * 0.5 * (width_mid + width_high))

    def along_x(values_in):
        return (interior(values_in, 1, 0, 0) - interior(values_in, -1, 0, 0)) / centre_span

    def along_y(values_in):
        return (interior(values_in, 0, 1, 0) - interior(values_in, 0, -1, 0)) * (0.5 / lateral_step)

    def along_z(values_in):
        return (interior(values_in, 0, 0, 1) - interior(values_in, 0, 0, -1)) * (0.5 / vertical_step)

    def lateral(values_in):
        centre_value = interior(values_in, 0, 0, 0)
        total = jnp.zeros_like(centre_value)
        for offset_y, offset_z, spacing in ((1, 0, lateral_step), (0, 1, vertical_step)):
            high_visc = 0.5 * (visc_mid + interior(viscous, 0, offset_y, offset_z))
            low_visc = 0.5 * (visc_mid + interior(viscous, 0, -offset_y, -offset_z))
            high_value = interior(values_in, 0, offset_y, offset_z)
            low_value = interior(values_in, 0, -offset_y, -offset_z)
            total = total + (high_visc * (high_value - centre_value) - low_visc * (centre_value - low_value)) / (spacing * spacing)
        return total

    half_y = 0.5 / lateral_step
    half_z = 0.5 / vertical_step
    flux_vx = viscous[1:-1] * (v_all[2:] - v_all[:-2]) / centre_span
    flux_wx = viscous[1:-1] * (w_all[2:] - w_all[:-2]) / centre_span
    cross_u = (flux_vx[:, 2:, 1:-1] - flux_vx[:, :-2, 1:-1]) * half_y + (flux_wx[:, 1:-1, 2:] - flux_wx[:, 1:-1, :-2]) * half_z
    flux_uy = viscous[:, 1:-1] * (u_all[:, 2:] - u_all[:, :-2]) * half_y
    flux_wy = viscous[:, 1:-1] * (w_all[:, 2:] - w_all[:, :-2]) * half_y
    cross_v = (flux_uy[2:, :, 1:-1] - flux_uy[:-2, :, 1:-1]) / centre_span + (flux_wy[1:-1, :, 2:] - flux_wy[1:-1, :, :-2]) * half_z
    flux_uz = viscous[:, :, 1:-1] * (u_all[:, :, 2:] - u_all[:, :, :-2]) * half_z
    flux_vz = viscous[:, :, 1:-1] * (v_all[:, :, 2:] - v_all[:, :, :-2]) * half_z
    cross_w = (flux_uz[2:, 1:-1] - flux_uz[:-2, 1:-1]) / centre_span + (flux_vz[1:-1, 2:] - flux_vz[1:-1, :-2]) * half_y

    u_mid = interior(u_all, 0, 0, 0)
    v_mid = interior(v_all, 0, 0, 0)
    w_mid = interior(w_all, 0, 0, 0)
    sides = []
    for values_in, cross_term in ((u_all, cross_u), (v_all, cross_v), (w_all, cross_w)):
        advect = -(u_mid * along_x(values_in) + v_mid * along_y(values_in) + w_mid * along_z(values_in))
        sides.append(interior(values_in, 0, 0, 0) + time_step * (advect + lateral(values_in) + cross_term))
    return jnp.stack(sides, axis=1), below_coef, above_coef


def reference(u_velocity, v_velocity, w_velocity, viscosity, cell_width):
    stacked = jnp.stack([u_velocity, v_velocity, w_velocity, viscosity])
    padded = jnp.pad(stacked, ((0, 0), (1, 1), (1, 1), (1, 1)))
    widths = jnp.pad(cell_width, 1)
    right_side, below_coef, above_coef = explicit_terms(padded, widths)
    diagonal = 1.0 + below_coef + above_coef
    solved = thomas(-below_coef, diagonal, -above_coef, right_side)
    return solved[:, 0], solved[:, 1], solved[:, 2]
```

```python
import functools

import jax
import jax.numpy as jnp
from jax import lax
from jax.experimental import pallas as pl
from jax.experimental.pallas import tpu as pltpu
from jax.sharding import PartitionSpec as P

time_step = 0.0125
face_factor = 2.0

LANES = 128
ROWS = 8
PAD = 8
FIELDS = 4
MESH = pl.DeviceIdType.MESH


def kernel(
    nx, ny,
    u_ref, v_ref, w_ref, nu_ref, width_ref,
    u_out, v_out, w_out,
    F, wv, span_inv, below_c, above_c, XH, ES, ER, CR, V, TP, PR, PS, SR, SS, O,
    local_sem, x_send, x_recv, y_send, y_recv, c_send, c_recv, w_send, w_recv,
    p_send, p_recv, s_send, s_recv, o_sem,
):
    X, Y, Z = u_ref.shape
    T = Z // LANES
    chunks = Y // ROWS
    gx = lax.axis_index("gx")
    gy = lax.axis_index("gy")
    has_x = (gx > 0, gx < nx - 1)
    has_y = (gy > 0, gy < ny - 1)
    inputs = (u_ref, v_ref, w_ref, nu_ref)
    outputs = (u_out, v_out, w_out)

    def local_copies():
        return [
            pltpu.make_async_copy(
                inputs[f].at[:, :, t * LANES:(t + 1) * LANES],
                F.at[f, 1:X + 1, t, PAD:PAD + Y, :],
                local_sem.at[f, t],
            )
            for f in range(FIELDS) for t in range(T)
        ]

    for copy in local_copies():
        copy.start()

    barrier = pltpu.get_barrier_semaphore()
    partners = []
    for dx in (-1, 0, 1):
        for dy in (-1, 0, 1):
            if dx == 0 and dy == 0:
                continue
            ok = None
            if dx:
                ok = has_x[(dx + 1) // 2]
            if dy:
                oky = has_y[(dy + 1) // 2]
                ok = oky if ok is None else jnp.logical_and(ok, oky)
            partners.append((dx, dy, ok))
    for dx, dy, ok in partners:
        @pl.when(ok)
        def _():
            pl.semaphore_signal(barrier, inc=1, device_id=(gx + dx, gy + dy), device_id_type=MESH)
    near_x = has_x[0].astype(jnp.int32) + has_x[1].astype(jnp.int32)
    near_y = has_y[0].astype(jnp.int32) + has_y[1].astype(jnp.int32)
    pl.semaphore_wait(barrier, near_x + near_y + near_x * near_y)

    def x_copy(s, f):
        return pltpu.make_async_remote_copy(
            src_ref=inputs[f].at[(X - 1) * s],
            dst_ref=XH.at[1 - s, f],
            send_sem=x_send.at[s, f], recv_sem=x_recv.at[1 - s, f],
            device_id=(gx + 2 * s - 1, gy), device_id_type=MESH,
        )

    def w_copy(s):
        return pltpu.make_async_remote_copy(
            src_ref=wv.at[X if s else 1],
            dst_ref=wv.at[0 if s else X + 1],
            send_sem=w_send.at[s], recv_sem=w_recv.at[1 - s],
            device_id=(gx + 2 * s - 1, gy), device_id_type=MESH,
        )

    def y_copy(s):
        return pltpu.make_async_remote_copy(
            src_ref=ES.at[s], dst_ref=ER.at[1 - s],
            send_sem=y_send.at[s], recv_sem=y_recv.at[1 - s],
            device_id=(gx, gy + 2 * s - 1), device_id_type=MESH,
        )

    def c_copy(a, b):
        return pltpu.make_async_remote_copy(
            src_ref=ES.at[b, 0:2, (X - 1) * a], dst_ref=CR.at[1 - a, 1 - b],
            send_sem=c_send.at[a, b], recv_sem=c_recv.at[1 - a, 1 - b],
            device_id=(gx + 2 * a - 1, gy + 2 * b - 1), device_id_type=MESH,
        )

    for s in (0, 1):
        @pl.when(has_x[s])
        def _():
            for f in range(FIELDS):
                x_copy(s, f).start()

    for i in range(X):
        wv[i + 1] = jnp.full((ROWS, LANES), width_ref[i], jnp.float32)
    for s in (0, 1):
        @pl.when(has_x[s])
        def _():
            w_copy(s).start()

        @pl.when(jnp.logical_not(has_x[s]))
        def _():
            wv[(X + 1) * s] = jnp.zeros((ROWS, LANES), jnp.float32)

    for copy in local_copies():
        copy.wait()

    edge = (PAD, PAD + Y - 1)
    outer = (PAD - 1, PAD + Y)

    def pack(f, carry):
        for s in (0, 1):
            ES[s, f] = F[f, 1:X + 1, :, edge[s]:edge[s] + 1, :]
        return carry

    lax.fori_loop(0, FIELDS, pack, 0)
    for s in (0, 1):
        @pl.when(has_y[s])
        def _():
            y_copy(s).start()
    for a in (0, 1):
        for b in (0, 1):
            @pl.when(jnp.logical_and(has_x[a], has_y[b]))
            def _():
                c_copy(a, b).start()

    for s in (0, 1):
        @pl.when(jnp.logical_not(has_y[s]))
        def _():
            def fill(f, carry):
                F[f, :, :, outer[s]:outer[s] + 1, :] = jnp.zeros((X + 2, T, 1, LANES), jnp.float32)
                return carry
            lax.fori_loop(0, FIELDS, fill, 0)

        @pl.when(jnp.logical_not(has_x[s]))
        def _():
            def fill(f, carry):
                F[f, (X + 1) * s] = jnp.zeros((T, Y + 2 * PAD, LANES), jnp.float32)
                return carry
            lax.fori_loop(0, FIELDS, fill, 0)

    for s in (0, 1):
        @pl.when(has_x[s])
        def _():
            w_copy(s).wait_send()
            w_copy(1 - s).wait_recv()
            for f in range(FIELDS):
                x_copy(s, f).wait_send()
                x_copy(1 - s, f).wait_recv()

            def spread(f, carry):
                for t in range(T):
                    F[f, (X + 1) * s, t, PAD:PAD + Y, :] = XH[s, f, :, t * LANES:(t + 1) * LANES]
                return carry
            lax.fori_loop(0, FIELDS, spread, 0)

    for i in range(X):
        low, mid, high = wv[i], wv[i + 1], wv[i + 2]
        span_inv[i] = 1.0 / (0.5 * low + mid + 0.5 * high)
        below_c[i] = time_step / (mid * (low + mid))
        above_c[i] = time_step / (mid * (mid + high))

    lane = lax.broadcasted_iota(jnp.int32, (T, ROWS, LANES), 2)
    first_lane = lane == 0
    last_lane = lane == LANES - 1
    zero_tile = jnp.zeros((1, ROWS, LANES), jnp.float32)

    def z_next(a):
        r = pltpu.roll(a, LANES - 1, 2)
        after = jnp.concatenate([r[1:], zero_tile], axis=0)
        return jnp.where(last_lane, after, r)

    def z_prev(a):
        r = pltpu.roll(a, 1, 2)
        before = jnp.concatenate([zero_tile, r[:-1]], axis=0)
        return jnp.where(first_lane, before, r)

    def z_diff(a):
        return z_next(a) - z_prev(a)

    def compute_chunk(yc):
        base = PAD + yc * ROWS

        def ld(f, i, dy=0):
            return F[f, i, :, pl.ds(base + dy, ROWS), :]

        def flux_uy(i):
            return ld(3, i) * (ld(0, i, 1) - ld(0, i, -1))

        def row(i, state):
            (fuy_prev, fuy_now, fuz_prev, fuz_now, u_zn, u_zp,
             c, v0, v1, v2, l, f0, f1, f2, fl, fr) = state
            inv_s = span_inv[i][None]
            nu0, nu_xp, nu_xm = ld(3, i + 1), ld(3, i + 2), ld(3, i)
            nu_yp, nu_ym = ld(3, i + 1, 1), ld(3, i + 1, -1)
            u_next_row = ld(0, i + 2)
            u_zn_next, u_zp_next = z_next(u_next_row), z_prev(u_next_row)
            fuy_next = flux_uy(i + 2)
            fuz_next = nu_xp * (u_zn_next - u_zp_next)

            face_yp, face_ym = nu0 + nu_yp, nu0 + nu_ym
            face_zp, face_zm = nu0 + z_next(nu0), nu0 + z_prev(nu0)
            face_sum = (face_yp + face_ym) + (face_zp + face_zm)
            mid = [ld(f, i + 1) for f in range(3)]
            u_scaled = mid[0] * inv_s

            x_dw = ld(2, i + 2) - ld(2, i)
            v_yp, v_ym = ld(1, i + 1, 1), ld(1, i + 1, -1)
            w_yp, w_ym = ld(2, i + 1, 1), ld(2, i + 1, -1)
            cross_u = inv_s * (
                nu_yp * (ld(1, i + 2, 1) - ld(1, i, 1))
                - nu_ym * (ld(1, i + 2, -1) - ld(1, i, -1))
                + z_diff(nu0 * x_dw)
            )
            cross_v = inv_s * (fuy_next - fuy_prev) + z_diff(nu0 * (w_yp - w_ym))
            cross_w = inv_s * (fuz_next - fuz_prev) + (nu_yp * z_diff(v_yp) - nu_ym * z_diff(v_ym))

            def side(f, cross, yp, ym, zn, zp, x_d):
                q = mid[f]
                advect = u_scaled * x_d + mid[1] * (yp - ym) + mid[2] * (zn - zp)
                spread = (face_yp * yp + face_ym * ym) + (face_zp * zn + face_zm * zp) - face_sum * q
                return q + time_step * (face_factor * spread + (cross - advect))

            r0 = side(0, cross_u, ld(0, i + 1, 1), ld(0, i + 1, -1), u_zn, u_zp, u_next_row - ld(0, i))
            r1 = side(1, cross_v, v_yp, v_ym, z_next(mid[1]), z_prev(mid[1]), ld(1, i + 2) - ld(1, i))
            r2 = side(2, cross_w, w_yp, w_ym, z_next(mid[2]), z_prev(mid[2]), x_dw)

            below = below_c[i][None] * (nu0 + nu_xm)
            above = above_c[i][None] * (nu0 + nu_xp)
            inv = 1.0 / (1.0 + above + below * (1.0 - c))
            c = above * inv
            lower = below * inv
            v0 = r0 * inv + lower * v0
            v1 = r1 * inv + lower * v1
            v2 = r2 * inv + lower * v2
            l = lower * l
            for k, value in enumerate((v0, v1, v2, l, c)):
                V[k, yc, i] = value
            f0 = f0 + fr * v0
            f1 = f1 + fr * v1
            f2 = f2 + fr * v2
            fl = fl + fr * l
            fr = fr * c
            return (fuy_now, fuy_next, fuz_now, fuz_next, u_zn_next, u_zp_next,
                    c, v0, v1, v2, l, f0, f1, f2, fl, fr)

        u_low, u_mid = ld(0, 0), ld(0, 1)
        u_zn, u_zp = z_next(u_mid), z_prev(u_mid)
        zero = jnp.zeros((T, ROWS, LANES), jnp.float32)
        one = jnp.ones((T, ROWS, LANES), jnp.float32)
        state = (flux_uy(0), flux_uy(1), ld(3, 0) * z_diff(u_low), ld(3, 1) * (u_zn - u_zp), u_zn, u_zp,
                 zero, zero, zero, zero, one, zero, zero, zero, zero, one)
        state = lax.fori_loop(0, X, row, state)
        c, v0, v1, v2, l, f0, f1, f2, fl, fr = state[6:]
        for k, value in enumerate((f0, f1, f2, fl, fr, v0, v1, v2, l, c)):
            TP[yc, k] = value

    def inner(k, carry):
        compute_chunk(k)
        return carry

    if chunks > 2:
        lax.fori_loop(1, chunks - 1, inner, 0)

    for s in (0, 1):
        @pl.when(has_y[s])
        def _():
            y_copy(s).wait_send()
            y_copy(1 - s).wait_recv()

            def spread(f, carry):
                F[f, 1:X + 1, :, outer[s]:outer[s] + 1, :] = ER[s, f]
                return carry
            lax.fori_loop(0, FIELDS, spread, 0)
    for a in (0, 1):
        for b in (0, 1):
            @pl.when(jnp.logical_and(has_x[a], has_y[b]))
            def _():
                c_copy(a, b).wait_send()
                c_copy(1 - a, 1 - b).wait_recv()
                for f in (0, 1):
                    F[f, (X + 1) * a, :, outer[b]:outer[b] + 1, :] = CR[a, b, f]

    ends = min(2, chunks)

    def outermost(k, carry):
        compute_chunk(k * (chunks - 1))
        return carry

    lax.fori_loop(0, ends, outermost, 0)

    def p_copy(yc):
        return pltpu.make_async_remote_copy(
            src_ref=PS.at[yc], dst_ref=PR.at[yc],
            send_sem=p_send.at[yc], recv_sem=p_recv.at[yc],
            device_id=(gx + 1, gy), device_id_type=MESH,
        )

    def s_copy(yc):
        return pltpu.make_async_remote_copy(
            src_ref=SS.at[yc], dst_ref=SR.at[yc],
            send_sem=s_send.at[yc], recv_sem=s_recv.at[yc],
            device_id=(gx - 1, gy), device_id_type=MESH,
        )

    @pl.when(gx == 0)
    def _():
        PR[...] = jnp.zeros(PR.shape, jnp.float32)

    @pl.when(gx == nx - 1)
    def _():
        SR[...] = jnp.zeros(SR.shape, jnp.float32)

    def relate(yc, came, give, near, far):
        near0, near_own, near_other = near
        far0, far_own, far_other = far
        q = came[yc, 3]
        own = TP[yc, near_own]
        m = q / (1.0 - own * q)
        gain = TP[yc, far_own]
        for k in range(3):
            p = came[yc, k]
            give[yc, k] = TP[yc, far0 + k] + gain * (p + m * (TP[yc, near0 + k] + own * p))
        give[yc, 3] = TP[yc, far_other] + gain * m * TP[yc, near_other]

    def back(yc):
        t_p, q_p = SR[yc, 3], PS[yc, 3]
        t_s, q_s = PR[yc, 3], SS[yc, 3]
        high_inv = 1.0 / (1.0 - t_p * q_p)
        low_inv = 1.0 / (1.0 - t_s * q_s)
        high = [(SR[yc, k] + t_p * PS[yc, k]) * high_inv for k in range(3)]
        low = [(PR[yc, k] + t_s * SS[yc, k]) * low_inv for k in range(3)]

        def row(n, now):
            i = X - 1 - n
            l, c = V[3, yc, i], V[4, yc, i]
            now = tuple(V[k, yc, i] + l * low[k] + c * now[k] for k in range(3))
            for k in range(3):
                for t in range(T):
                    O[k, i, pl.ds(pl.multiple_of(yc * ROWS, ROWS), ROWS), t * LANES:(t + 1) * LANES] = now[k][t]
            return now

        lax.fori_loop(0, X, row, tuple(high))
        for k in range(3):
            out_copy(k, yc).start()

    def out_copy(k, yc):
        part = pl.ds(pl.multiple_of(yc * ROWS, ROWS), ROWS)
        return pltpu.make_async_copy(O.at[k, :, part, :], outputs[k].at[:, part, :], o_sem.at[k, yc])

    def link_step(step, carry):
        up = step - gx
        down = step - (nx - 1 - gx)

        @pl.when(jnp.logical_and(up >= 0, up < chunks))
        def _():
            @pl.when(has_x[0])
            def _():
                p_copy(up).wait_recv()
            relate(up, PR, PS, (0, 3, 4), (5, 8, 9))

            @pl.when(has_x[1])
            def _():
                p_copy(up).start()

        @pl.when(jnp.logical_and(down >= 0, down < chunks))
        def _():
            @pl.when(has_x[1])
            def _():
                s_copy(down).wait_recv()
            relate(down, SR, SS, (5, 9, 8), (0, 4, 3))

            @pl.when(has_x[0])
            def _():
                s_copy(down).start()

        ready = step - (nx - 1)

        @pl.when(ready >= 0)
        def _():
            back(ready)

        return carry

    lax.fori_loop(0, nx - 1 + chunks, link_step, 0)

    for yc in range(chunks):
        @pl.when(has_x[1])
        def _():
            p_copy(yc).wait_send()

        @pl.when(has_x[0])
        def _():
            s_copy(yc).wait_send()
        for k in range(3):
            out_copy(k, yc).wait()


def per_device(nx, ny, u_velocity, v_velocity, w_velocity, viscosity, cell_width):
    X, Y, Z = u_velocity.shape
    T = Z // LANES
    chunks = Y // ROWS
    f32 = jnp.float32
    dma = pltpu.SemaphoreType.DMA
    anywhere = pl.BlockSpec(memory_space=pl.ANY)
    out = jax.ShapeDtypeStruct((X, Y, Z), f32)
    return pl.pallas_call(
        functools.partial(kernel, nx, ny),
        out_shape=(out, out, out),
        in_specs=[anywhere] * 4 + [pl.BlockSpec(memory_space=pltpu.SMEM)],
        out_specs=(anywhere,) * 3,
        scratch_shapes=[
            pltpu.VMEM((FIELDS, X + 2, T, Y + 2 * PAD, LANES), f32),
            pltpu.VMEM((X + 2, ROWS, LANES), f32),
            pltpu.VMEM((X, ROWS, LANES), f32),
            pltpu.VMEM((X, ROWS, LANES), f32),
            pltpu.VMEM((X, ROWS, LANES), f32),
            pltpu.VMEM((2, FIELDS, Y, Z), f32),
            pltpu.VMEM((2, FIELDS, X, T, 1, LANES), f32),
            pltpu.VMEM((2, FIELDS, X, T, 1, LANES), f32),
            pltpu.VMEM((2, 2, 2, T, 1, LANES), f32),
            pltpu.VMEM((5, chunks, X, T, ROWS, LANES), f32),
            pltpu.VMEM((chunks, 10, T, ROWS, LANES), f32),
            pltpu.VMEM((chunks, 4, T, ROWS, LANES), f32),
            pltpu.VMEM((chunks, 4, T, ROWS, LANES), f32),
            pltpu.VMEM((chunks, 4, T, ROWS, LANES), f32),
            pltpu.VMEM((chunks, 4, T, ROWS, LANES), f32),
            pltpu.VMEM((3, X, Y, Z), f32),
            dma((FIELDS, T)),
            dma((2, FIELDS)), dma((2, FIELDS)),
            dma((2,)), dma((2,)),
            dma((2, 2)), dma((2, 2)),
            dma((2,)), dma((2,)),
            dma((chunks,)), dma((chunks,)),
            dma((chunks,)), dma((chunks,)),
            dma((3, chunks)),
        ],
        compiler_params=pltpu.CompilerParams(
            collective_id=0, has_side_effects=True, vmem_limit_bytes=48 * 1024 * 1024
        ),
    )(u_velocity, v_velocity, w_velocity, viscosity, cell_width)


def solution(mesh):
    spec = P("gx", "gy", None)
    return jax.shard_map(
        functools.partial(per_device, mesh.shape["gx"], mesh.shape["gy"]),
        mesh=mesh,
        in_specs=(spec, spec, spec, spec, P("gx")),
        out_specs=(spec, spec, spec),
        check_vma=False,
    )
```

```python
import functools

import jax
import jax.numpy as jnp
from jax import lax
from jax.experimental import pallas as pl
from jax.experimental.pallas import tpu as pltpu
from jax.sharding import PartitionSpec as P

time_step = 0.0125
face_factor = 2.0

LANES = 128
ROWS = 8
PAD = 8
FIELDS = 4
MESH = pl.DeviceIdType.MESH


def kernel(
    nx, ny,
    u_ref, v_ref, w_ref, nu_ref, width_in,
    V, ends_out,
    F, wv, span_inv, below_c, above_c, XH, ES, ER, CR, TP, PR, PS, SR, SS, width_ref,
    width_sem, local_sem, x_send, x_recv, y_send, y_recv, c_send, c_recv, w_send, w_recv,
    p_send, p_recv, s_send, s_recv,
):
    X, Y, Z = u_ref.shape
    T = Z // LANES
    chunks = Y // ROWS
    gx = lax.axis_index("gx")
    gy = lax.axis_index("gy")
    has_x = (gx > 0, gx < nx - 1)
    has_y = (gy > 0, gy < ny - 1)
    inputs = (u_ref, v_ref, w_ref, nu_ref)

    def local_copies():
        return [
            pltpu.make_async_copy(
                inputs[f].at[:, :, t * LANES:(t + 1) * LANES],
                F.at[f, 1:X + 1, t, PAD:PAD + Y, :],
                local_sem.at[f, t],
            )
            for f in range(FIELDS) for t in range(T)
        ]

    width_copy = pltpu.make_async_copy(width_in, width_ref, width_sem)
    width_copy.start()
    for copy in local_copies():
        copy.start()

    barrier = pltpu.get_barrier_semaphore()
    partners = []
    for dx in (-1, 0, 1):
        for dy in (-1, 0, 1):
            if dx == 0 and dy == 0:
                continue
            ok = None
            if dx:
                ok = has_x[(dx + 1) // 2]
            if dy:
                oky = has_y[(dy + 1) // 2]
                ok = oky if ok is None else jnp.logical_and(ok, oky)
            partners.append((dx, dy, ok))
    for dx, dy, ok in partners:
        @pl.when(ok)
        def _():
            pl.semaphore_signal(barrier, inc=1, device_id=(gx + dx, gy + dy), device_id_type=MESH)
    near_x = has_x[0].astype(jnp.int32) + has_x[1].astype(jnp.int32)
    near_y = has_y[0].astype(jnp.int32) + has_y[1].astype(jnp.int32)
    pl.semaphore_wait(barrier, near_x + near_y + near_x * near_y)

    def x_copy(s, f):
        return pltpu.make_async_remote_copy(
            src_ref=inputs[f].at[(X - 1) * s],
            dst_ref=XH.at[1 - s, f],
            send_sem=x_send.at[s, f], recv_sem=x_recv.at[1 - s, f],
            device_id=(gx + 2 * s - 1, gy), device_id_type=MESH,
        )

    def w_copy(s):
        return pltpu.make_async_remote_copy(
            src_ref=wv.at[X if s else 1],
            dst_ref=wv.at[0 if s else X + 1],
            send_sem=w_send.at[s], recv_sem=w_recv.at[1 - s],
            device_id=(gx + 2 * s - 1, gy), device_id_type=MESH,
        )

    def y_copy(s):
        return pltpu.make_async_remote_copy(
            src_ref=ES.at[s], dst_ref=ER.at[1 - s],
            send_sem=y_send.at[s], recv_sem=y_recv.at[1 - s],
            device_id=(gx, gy + 2 * s - 1), device_id_type=MESH,
        )

    def c_copy(a, b):
        return pltpu.make_async_remote_copy(
            src_ref=ES.at[b, 0:2, (X - 1) * a], dst_ref=CR.at[1 - a, 1 - b],
            send_sem=c_send.at[a, b], recv_sem=c_recv.at[1 - a, 1 - b],
            device_id=(gx + 2 * a - 1, gy + 2 * b - 1), device_id_type=MESH,
        )

    for s in (0, 1):
        @pl.when(has_x[s])
        def _():
            for f in range(FIELDS):
                x_copy(s, f).start()

    width_copy.wait()
    for i in range(X):
        wv[i + 1] = jnp.full((ROWS, LANES), width_ref[i], jnp.float32)
    for s in (0, 1):
        @pl.when(has_x[s])
        def _():
            w_copy(s).start()

        @pl.when(jnp.logical_not(has_x[s]))
        def _():
            wv[(X + 1) * s] = jnp.zeros((ROWS, LANES), jnp.float32)

    for copy in local_copies():
        copy.wait()

    edge = (PAD, PAD + Y - 1)
    outer = (PAD - 1, PAD + Y)

    def pack(f, carry):
        for s in (0, 1):
            ES[s, f] = F[f, 1:X + 1, :, edge[s]:edge[s] + 1, :]
        return carry

    lax.fori_loop(0, FIELDS, pack, 0)
    for s in (0, 1):
        @pl.when(has_y[s])
        def _():
            y_copy(s).start()
    for a in (0, 1):
        for b in (0, 1):
            @pl.when(jnp.logical_and(has_x[a], has_y[b]))
            def _():
                c_copy(a, b).start()

    for s in (0, 1):
        @pl.when(jnp.logical_not(has_y[s]))
        def _():
            def fill(f, carry):
                F[f, :, :, outer[s]:outer[s] + 1, :] = jnp.zeros((X + 2, T, 1, LANES), jnp.float32)
                return carry
            lax.fori_loop(0, FIELDS, fill, 0)

        @pl.when(jnp.logical_not(has_x[s]))
        def _():
            def fill(f, carry):
                F[f, (X + 1) * s] = jnp.zeros((T, Y + 2 * PAD, LANES), jnp.float32)
                return carry
            lax.fori_loop(0, FIELDS, fill, 0)

    for s in (0, 1):
        @pl.when(has_x[s])
        def _():
            w_copy(s).wait_send()
            w_copy(1 - s).wait_recv()
            for f in range(FIELDS):
                x_copy(s, f).wait_send()
                x_copy(1 - s, f).wait_recv()

            def spread(f, carry):
                for t in range(T):
                    F[f, (X + 1) * s, t, PAD:PAD + Y, :] = XH[s, f, :, t * LANES:(t + 1) * LANES]
                return carry
            lax.fori_loop(0, FIELDS, spread, 0)

    for i in range(X):
        low, mid, high = wv[i], wv[i + 1], wv[i + 2]
        span_inv[i] = 1.0 / (0.5 * low + mid + 0.5 * high)
        below_c[i] = time_step / (mid * (low + mid))
        above_c[i] = time_step / (mid * (mid + high))

    lane = lax.broadcasted_iota(jnp.int32, (T, ROWS, LANES), 2)
    first_lane = lane == 0
    last_lane = lane == LANES - 1
    zero_tile = jnp.zeros((1, ROWS, LANES), jnp.float32)

    def z_next(a):
        r = pltpu.roll(a, LANES - 1, 2)
        after = jnp.concatenate([r[1:], zero_tile], axis=0)
        return jnp.where(last_lane, after, r)

    def z_prev(a):
        r = pltpu.roll(a, 1, 2)
        before = jnp.concatenate([zero_tile, r[:-1]], axis=0)
        return jnp.where(first_lane, before, r)

    def z_diff(a):
        return z_next(a) - z_prev(a)

    def compute_chunk(yc):
        base = PAD + yc * ROWS

        def ld(f, i, dy=0):
            return F[f, i, :, pl.ds(base + dy, ROWS), :]

        def flux_uy(i):
            return ld(3, i) * (ld(0, i, 1) - ld(0, i, -1))

        def row(i, state):
            (fuy_prev, fuy_now, fuz_prev, fuz_now, u_zn, u_zp,
             c, v0, v1, v2, l, f0, f1, f2, fl, fr) = state
            inv_s = span_inv[i][None]
            nu0, nu_xp, nu_xm = ld(3, i + 1), ld(3, i + 2), ld(3, i)
            nu_yp, nu_ym = ld(3, i + 1, 1), ld(3, i + 1, -1)
            u_next_row = ld(0, i + 2)
            u_zn_next, u_zp_next = z_next(u_next_row), z_prev(u_next_row)
            fuy_next = flux_uy(i + 2)
            fuz_next = nu_xp * (u_zn_next - u_zp_next)

            face_yp, face_ym = nu0 + nu_yp, nu0 + nu_ym
            face_zp, face_zm = nu0 + z_next(nu0), nu0 + z_prev(nu0)
            face_sum = (face_yp + face_ym) + (face_zp + face_zm)
            mid = [ld(f, i + 1) for f in range(3)]
            u_scaled = mid[0] * inv_s

            x_dw = ld(2, i + 2) - ld(2, i)
            v_yp, v_ym = ld(1, i + 1, 1), ld(1, i + 1, -1)
            w_yp, w_ym = ld(2, i + 1, 1), ld(2, i + 1, -1)
            cross_u = inv_s * (
                nu_yp * (ld(1, i + 2, 1) - ld(1, i, 1))
                - nu_ym * (ld(1, i + 2, -1) - ld(1, i, -1))
                + z_diff(nu0 * x_dw)
            )
            cross_v = inv_s * (fuy_next - fuy_prev) + z_diff(nu0 * (w_yp - w_ym))
            cross_w = inv_s * (fuz_next - fuz_prev) + (nu_yp * z_diff(v_yp) - nu_ym * z_diff(v_ym))

            def side(f, cross, yp, ym, zn, zp, x_d):
                q = mid[f]
                advect = u_scaled * x_d + mid[1] * (yp - ym) + mid[2] * (zn - zp)
                spread = (face_yp * yp + face_ym * ym) + (face_zp * zn + face_zm * zp) - face_sum * q
                return q + time_step * (face_factor * spread + (cross - advect))

            r0 = side(0, cross_u, ld(0, i + 1, 1), ld(0, i + 1, -1), u_zn, u_zp, u_next_row - ld(0, i))
            r1 = side(1, cross_v, v_yp, v_ym, z_next(mid[1]), z_prev(mid[1]), ld(1, i + 2) - ld(1, i))
            r2 = side(2, cross_w, w_yp, w_ym, z_next(mid[2]), z_prev(mid[2]), x_dw)

            below = below_c[i][None] * (nu0 + nu_xm)
            above = above_c[i][None] * (nu0 + nu_xp)
            inv = 1.0 / (1.0 + above + below * (1.0 - c))
            c = above * inv
            lower = below * inv
            v0 = r0 * inv + lower * v0
            v1 = r1 * inv + lower * v1
            v2 = r2 * inv + lower * v2
            l = lower * l
            for k, value in enumerate((v0, v1, v2, l, c)):
                V[k, yc, i] = value
            f0 = f0 + fr * v0
            f1 = f1 + fr * v1
            f2 = f2 + fr * v2
            fl = fl + fr * l
            fr = fr * c
            return (fuy_now, fuy_next, fuz_now, fuz_next, u_zn_next, u_zp_next,
                    c, v0, v1, v2, l, f0, f1, f2, fl, fr)

        u_low, u_mid = ld(0, 0), ld(0, 1)
        u_zn, u_zp = z_next(u_mid), z_prev(u_mid)
        zero = jnp.zeros((T, ROWS, LANES), jnp.float32)
        one = jnp.ones((T, ROWS, LANES), jnp.float32)
        state = (flux_uy(0), flux_uy(1), ld(3, 0) * z_diff(u_low), ld(3, 1) * (u_zn - u_zp), u_zn, u_zp,
                 zero, zero, zero, zero, one, zero, zero, zero, zero, one)
        state = lax.fori_loop(0, X, row, state)
        c, v0, v1, v2, l, f0, f1, f2, fl, fr = state[6:]
        for k, value in enumerate((f0, f1, f2, fl, fr, v0, v1, v2, l, c)):
            TP[yc, k] = value

    def inner(k, carry):
        compute_chunk(k)
        return carry

    if chunks > 2:
        lax.fori_loop(1, chunks - 1, inner, 0)

    for s in (0, 1):
        @pl.when(has_y[s])
        def _():
            y_copy(s).wait_send()
            y_copy(1 - s).wait_recv()

            def spread(f, carry):
                F[f, 1:X + 1, :, outer[s]:outer[s] + 1, :] = ER[s, f]
                return carry
            lax.fori_loop(0, FIELDS, spread, 0)
    for a in (0, 1):
        for b in (0, 1):
            @pl.when(jnp.logical_and(has_x[a], has_y[b]))
            def _():
                c_copy(a, b).wait_send()
                c_copy(1 - a, 1 - b).wait_recv()
                for f in (0, 1):
                    F[f, (X + 1) * a, :, outer[b]:outer[b] + 1, :] = CR[a, b, f]

    ends = min(2, chunks)

    def outermost(k, carry):
        compute_chunk(k * (chunks - 1))
        return carry

    lax.fori_loop(0, ends, outermost, 0)

    def p_copy(yc):
        return pltpu.make_async_remote_copy(
            src_ref=PS.at[yc], dst_ref=PR.at[yc],
            send_sem=p_send.at[yc], recv_sem=p_recv.at[yc],
            device_id=(gx + 1, gy), device_id_type=MESH,
        )

    def s_copy(yc):
        return pltpu.make_async_remote_copy(
            src_ref=SS.at[yc], dst_ref=SR.at[yc],
            send_sem=s_send.at[yc], recv_sem=s_recv.at[yc],
            device_id=(gx - 1, gy), device_id_type=MESH,
        )

    @pl.when(gx == 0)
    def _():
        PR[...] = jnp.zeros(PR.shape, jnp.float32)

    @pl.when(gx == nx - 1)
    def _():
        SR[...] = jnp.zeros(SR.shape, jnp.float32)

    def relate(yc, came, give, near, far):
        near0, near_own, near_other = near
        far0, far_own, far_other = far
        q = came[yc, 3]
        own = TP[yc, near_own]
        m = q / (1.0 - own * q)
        gain = TP[yc, far_own]
        for k in range(3):
            p = came[yc, k]
            give[yc, k] = TP[yc, far0 + k] + gain * (p + m * (TP[yc, near0 + k] + own * p))
        give[yc, 3] = TP[yc, far_other] + gain * m * TP[yc, near_other]

    def close(yc):
        t_p, q_p = SR[yc, 3], PS[yc, 3]
        t_s, q_s = PR[yc, 3], SS[yc, 3]
        high_inv = 1.0 / (1.0 - t_p * q_p)
        low_inv = 1.0 / (1.0 - t_s * q_s)
        for k in range(3):
            ends_out[yc, k] = (PR[yc, k] + t_s * SS[yc, k]) * low_inv
            ends_out[yc, 3 + k] = (SR[yc, k] + t_p * PS[yc, k]) * high_inv

    def pass_up(k, carry):
        @pl.when(has_x[0])
        def _():
            p_copy(k).wait_recv()
        relate(k, PR, PS, (0, 3, 4), (5, 8, 9))

        @pl.when(has_x[1])
        def _():
            p_copy(k).start()
        return carry

    def pass_down(k, carry):
        @pl.when(has_x[1])
        def _():
            s_copy(k).wait_recv()
        relate(k, SR, SS, (5, 9, 8), (0, 4, 3))

        @pl.when(has_x[0])
        def _():
            s_copy(k).start()
        return carry

    low_half = gx < nx // 2

    @pl.when(low_half)
    def _():
        lax.fori_loop(0, chunks, pass_up, 0)
        lax.fori_loop(0, chunks, pass_down, 0)

    @pl.when(jnp.logical_not(low_half))
    def _():
        lax.fori_loop(0, chunks, pass_down, 0)
        lax.fori_loop(0, chunks, pass_up, 0)

    def close_step(yc, carry):
        close(yc)
        return carry

    lax.fori_loop(0, chunks, close_step, 0)

    for yc in range(chunks):
        @pl.when(has_x[1])
        def _():
            p_copy(yc).wait_send()

        @pl.when(has_x[0])
        def _():
            s_copy(yc).wait_send()


def substitute(V, ends, u_out, v_out, w_out, O, o_sem):
    _, chunks, X, T, _, _ = V.shape
    outputs = (u_out, v_out, w_out)

    def copy(k, yc):
        part = pl.ds(pl.multiple_of(yc * ROWS, ROWS), ROWS)
        return pltpu.make_async_copy(O.at[k, :, part, :], outputs[k].at[:, part, :], o_sem.at[k, yc])

    def chunk(yc, carry):
        low = [ends[yc, k] for k in range(3)]

        def row(n, now):
            i = X - 1 - n
            l, c = V[3, yc, i], V[4, yc, i]
            now = tuple(V[k, yc, i] + l * low[k] + c * now[k] for k in range(3))
            for k in range(3):
                for t in range(T):
                    O[k, i, pl.ds(pl.multiple_of(yc * ROWS, ROWS), ROWS), t * LANES:(t + 1) * LANES] = now[k][t]
            return now

        lax.fori_loop(0, X, row, tuple(ends[yc, 3 + k] for k in range(3)))
        for k in range(3):
            copy(k, yc).start()
        return carry

    lax.fori_loop(0, chunks, chunk, 0)
    for yc in range(chunks):
        for k in range(3):
            copy(k, yc).wait()


def per_device(nx, ny, u_velocity, v_velocity, w_velocity, viscosity, cell_width):
    X, Y, Z = u_velocity.shape
    T = Z // LANES
    chunks = Y // ROWS
    f32 = jnp.float32
    dma = pltpu.SemaphoreType.DMA
    in_hbm = pl.BlockSpec(memory_space=pltpu.HBM)
    in_vmem = pl.BlockSpec(memory_space=pltpu.VMEM)
    out = jax.ShapeDtypeStruct((X, Y, Z), f32)
    rows, ends = pl.pallas_call(
        functools.partial(kernel, nx, ny),
        out_shape=(
            jax.ShapeDtypeStruct((5, chunks, X, T, ROWS, LANES), f32),
            jax.ShapeDtypeStruct((chunks, 6, T, ROWS, LANES), f32),
        ),
        in_specs=[in_hbm] * 5,
        out_specs=(in_vmem,) * 2,
        scratch_shapes=[
            pltpu.VMEM((FIELDS, X + 2, T, Y + 2 * PAD, LANES), f32),
            pltpu.VMEM((X + 2, ROWS, LANES), f32),
            pltpu.VMEM((X, ROWS, LANES), f32),
            pltpu.VMEM((X, ROWS, LANES), f32),
            pltpu.VMEM((X, ROWS, LANES), f32),
            pltpu.VMEM((2, FIELDS, Y, Z), f32),
            pltpu.VMEM((2, FIELDS, X, T, 1, LANES), f32),
            pltpu.VMEM((2, FIELDS, X, T, 1, LANES), f32),
            pltpu.VMEM((2, 2, 2, T, 1, LANES), f32),
            pltpu.VMEM((chunks, 10, T, ROWS, LANES), f32),
            pltpu.VMEM((chunks, 4, T, ROWS, LANES), f32),
            pltpu.VMEM((chunks, 4, T, ROWS, LANES), f32),
            pltpu.VMEM((chunks, 4, T, ROWS, LANES), f32),
            pltpu.VMEM((chunks, 4, T, ROWS, LANES), f32),
            pltpu.SMEM((X,), f32),
            dma, dma((FIELDS, T)),
            dma((2, FIELDS)), dma((2, FIELDS)),
            dma((2,)), dma((2,)),
            dma((2, 2)), dma((2, 2)),
            dma((2,)), dma((2,)),
            dma((chunks,)), dma((chunks,)),
            dma((chunks,)), dma((chunks,)),
        ],
        compiler_params=pltpu.CompilerParams(
            collective_id=0, has_side_effects=True, vmem_limit_bytes=57 * 1024 * 1024
        ),
    )(u_velocity, v_velocity, w_velocity, viscosity, cell_width)
    return pl.pallas_call(
        substitute,
        out_shape=(out, out, out),
        in_specs=[in_vmem] * 2,
        out_specs=(in_hbm,) * 3,
        scratch_shapes=[pltpu.VMEM((3, X, Y, Z), f32), dma((3, chunks))],
        compiler_params=pltpu.CompilerParams(vmem_limit_bytes=16 * 1024 * 1024),
    )(rows, ends)


def solution(mesh):
    spec = P("gx", "gy", None)
    return jax.shard_map(
        functools.partial(per_device, mesh.shape["gx"], mesh.shape["gy"]),
        mesh=mesh,
        in_specs=(spec, spec, spec, spec, P("gx")),
        out_specs=(spec, spec, spec),
        check_vma=False,
    )
```

```python
import functools

import jax
import jax.numpy as jnp
from jax import lax
from jax.experimental import pallas as pl
from jax.experimental.pallas import tpu as pltpu
from jax.sharding import PartitionSpec as P

time_step = 0.0125
face_factor = 2.0

LANES = 128
ROWS = 8
PAD = 8
FIELDS = 4
MESH = pl.DeviceIdType.MESH


def kernel(
    nx, ny,
    u_ref, v_ref, w_ref, nu_ref, width_in,
    V, ends_out,
    F, wv, span_inv, below_c, above_c, XH, ES, ER, CR, TP, PR, PS, SR, SS, width_ref,
    width_sem, local_sem, x_send, x_recv, y_send, y_recv, c_send, c_recv, w_send, w_recv,
    p_send, p_recv, s_send, s_recv,
):
    X, Y, Z = u_ref.shape
    T = Z // LANES
    chunks = Y // ROWS
    gx = lax.axis_index("gx")
    gy = lax.axis_index("gy")
    has_x = (gx > 0, gx < nx - 1)
    has_y = (gy > 0, gy < ny - 1)
    inputs = (u_ref, v_ref, w_ref, nu_ref)

    def local_copies():
        return [
            pltpu.make_async_copy(
                inputs[f].at[:, :, t * LANES:(t + 1) * LANES],
                F.at[f, 1:X + 1, t, PAD:PAD + Y, :],
                local_sem.at[f, t],
            )
            for f in range(FIELDS) for t in range(T)
        ]

    width_copy = pltpu.make_async_copy(width_in, width_ref, width_sem)
    width_copy.start()
    for copy in local_copies():
        copy.start()

    barrier = pltpu.get_barrier_semaphore()
    partners = []
    for dx in (-1, 0, 1):
        for dy in (-1, 0, 1):
            if dx == 0 and dy == 0:
                continue
            ok = None
            if dx:
                ok = has_x[(dx + 1) // 2]
            if dy:
                oky = has_y[(dy + 1) // 2]
                ok = oky if ok is None else jnp.logical_and(ok, oky)
            partners.append((dx, dy, ok))
    for dx, dy, ok in partners:
        @pl.when(ok)
        def _():
            pl.semaphore_signal(barrier, inc=1, device_id=(gx + dx, gy + dy), device_id_type=MESH)
    near_x = has_x[0].astype(jnp.int32) + has_x[1].astype(jnp.int32)
    near_y = has_y[0].astype(jnp.int32) + has_y[1].astype(jnp.int32)
    pl.semaphore_wait(barrier, near_x + near_y + near_x * near_y)

    def x_copy(s, f):
        return pltpu.make_async_remote_copy(
            src_ref=inputs[f].at[(X - 1) * s],
            dst_ref=XH.at[1 - s, f],
            send_sem=x_send.at[s, f], recv_sem=x_recv.at[1 - s, f],
            device_id=(gx + 2 * s - 1, gy), device_id_type=MESH,
        )

    def w_copy(s):
        return pltpu.make_async_remote_copy(
            src_ref=wv.at[X if s else 1],
            dst_ref=wv.at[0 if s else X + 1],
            send_sem=w_send.at[s], recv_sem=w_recv.at[1 - s],
            device_id=(gx + 2 * s - 1, gy), device_id_type=MESH,
        )

    def y_copy(s, f):
        return pltpu.make_async_remote_copy(
            src_ref=ES.at[s, f], dst_ref=ER.at[1 - s, f],
            send_sem=y_send.at[s, f], recv_sem=y_recv.at[1 - s, f],
            device_id=(gx, gy + 2 * s - 1), device_id_type=MESH,
        )

    def c_copy(a, b):
        return pltpu.make_async_remote_copy(
            src_ref=ES.at[b, 0:2, (X - 1) * a], dst_ref=CR.at[1 - a, 1 - b],
            send_sem=c_send.at[a, b], recv_sem=c_recv.at[1 - a, 1 - b],
            device_id=(gx + 2 * a - 1, gy + 2 * b - 1), device_id_type=MESH,
        )

    for s in (0, 1):
        @pl.when(has_x[s])
        def _():
            for f in range(FIELDS):
                x_copy(s, f).start()

    width_copy.wait()
    for i in range(X):
        wv[i + 1] = jnp.full((ROWS, LANES), width_ref[i], jnp.float32)
    for s in (0, 1):
        @pl.when(has_x[s])
        def _():
            w_copy(s).start()

        @pl.when(jnp.logical_not(has_x[s]))
        def _():
            wv[(X + 1) * s] = jnp.zeros((ROWS, LANES), jnp.float32)

    edge = (PAD, PAD + Y - 1)
    outer = (PAD - 1, PAD + Y)
    arriving = local_copies()
    for f in range(FIELDS):
        for copy in arriving[f * T:(f + 1) * T]:
            copy.wait()
        for s in (0, 1):
            @pl.when(has_y[s])
            def _():
                ES[s, f] = F[f, 1:X + 1, :, edge[s]:edge[s] + 1, :]
                y_copy(s, f).start()
    for a in (0, 1):
        for b in (0, 1):
            @pl.when(jnp.logical_and(has_x[a], has_y[b]))
            def _():
                c_copy(a, b).start()

    for s in (0, 1):
        @pl.when(jnp.logical_not(has_y[s]))
        def _():
            def fill(f, carry):
                F[f, :, :, outer[s]:outer[s] + 1, :] = jnp.zeros((X + 2, T, 1, LANES), jnp.float32)
                return carry
            lax.fori_loop(0, FIELDS, fill, 0)

        @pl.when(jnp.logical_not(has_x[s]))
        def _():
            def fill(f, carry):
                F[f, (X + 1) * s] = jnp.zeros((T, Y + 2 * PAD, LANES), jnp.float32)
                return carry
            lax.fori_loop(0, FIELDS, fill, 0)

    for s in (0, 1):
        @pl.when(has_x[s])
        def _():
            w_copy(s).wait_send()
            w_copy(1 - s).wait_recv()
            for f in range(FIELDS):
                x_copy(s, f).wait_send()
                x_copy(1 - s, f).wait_recv()

            def spread(f, carry):
                for t in range(T):
                    F[f, (X + 1) * s, t, PAD:PAD + Y, :] = XH[s, f, :, t * LANES:(t + 1) * LANES]
                return carry
            lax.fori_loop(0, FIELDS, spread, 0)

    for i in range(X):
        low, mid, high = wv[i], wv[i + 1], wv[i + 2]
        span_inv[i] = 1.0 / (0.5 * low + mid + 0.5 * high)
        below_c[i] = time_step / (mid * (low + mid))
        above_c[i] = time_step / (mid * (mid + high))

    lane = lax.broadcasted_iota(jnp.int32, (T, ROWS, LANES), 2)
    first_lane = lane == 0
    last_lane = lane == LANES - 1
    zero_tile = jnp.zeros((1, ROWS, LANES), jnp.float32)

    def z_next(a):
        r = pltpu.roll(a, LANES - 1, 2)
        after = jnp.concatenate([r[1:], zero_tile], axis=0)
        return jnp.where(last_lane, after, r)

    def z_prev(a):
        r = pltpu.roll(a, 1, 2)
        before = jnp.concatenate([zero_tile, r[:-1]], axis=0)
        return jnp.where(first_lane, before, r)

    def z_diff(a):
        return z_next(a) - z_prev(a)

    def compute_chunk(yc):
        base = PAD + yc * ROWS

        def ld(f, i, dy=0):
            return F[f, i, :, pl.ds(base + dy, ROWS), :]

        def flux_uy(i):
            return ld(3, i) * (ld(0, i, 1) - ld(0, i, -1))

        def row(i, state):
            (fuy_prev, fuy_now, fuz_prev, fuz_now, u_zn, u_zp,
             c, v0, v1, v2, l, f0, f1, f2, fl, fr) = state
            inv_s = span_inv[i][None]
            nu0, nu_xp, nu_xm = ld(3, i + 1), ld(3, i + 2), ld(3, i)
            nu_yp, nu_ym = ld(3, i + 1, 1), ld(3, i + 1, -1)
            u_next_row = ld(0, i + 2)
            u_zn_next, u_zp_next = z_next(u_next_row), z_prev(u_next_row)
            fuy_next = flux_uy(i + 2)
            fuz_next = nu_xp * (u_zn_next - u_zp_next)

            face_yp, face_ym = nu0 + nu_yp, nu0 + nu_ym
            face_zp, face_zm = nu0 + z_next(nu0), nu0 + z_prev(nu0)
            face_sum = (face_yp + face_ym) + (face_zp + face_zm)
            mid = [ld(f, i + 1) for f in range(3)]
            u_scaled = mid[0] * inv_s

            x_dw = ld(2, i + 2) - ld(2, i)
            v_yp, v_ym = ld(1, i + 1, 1), ld(1, i + 1, -1)
            w_yp, w_ym = ld(2, i + 1, 1), ld(2, i + 1, -1)
            cross_u = inv_s * (
                nu_yp * (ld(1, i + 2, 1) - ld(1, i, 1))
                - nu_ym * (ld(1, i + 2, -1) - ld(1, i, -1))
                + z_diff(nu0 * x_dw)
            )
            cross_v = inv_s * (fuy_next - fuy_prev) + z_diff(nu0 * (w_yp - w_ym))
            cross_w = inv_s * (fuz_next - fuz_prev) + (nu_yp * z_diff(v_yp) - nu_ym * z_diff(v_ym))

            def side(f, cross, yp, ym, zn, zp, x_d):
                q = mid[f]
                advect = u_scaled * x_d + mid[1] * (yp - ym) + mid[2] * (zn - zp)
                spread = (face_yp * yp + face_ym * ym) + (face_zp * zn + face_zm * zp) - face_sum * q
                return q + time_step * (face_factor * spread + (cross - advect))

            r0 = side(0, cross_u, ld(0, i + 1, 1), ld(0, i + 1, -1), u_zn, u_zp, u_next_row - ld(0, i))
            r1 = side(1, cross_v, v_yp, v_ym, z_next(mid[1]), z_prev(mid[1]), ld(1, i + 2) - ld(1, i))
            r2 = side(2, cross_w, w_yp, w_ym, z_next(mid[2]), z_prev(mid[2]), x_dw)

            below = below_c[i][None] * (nu0 + nu_xm)
            above = above_c[i][None] * (nu0 + nu_xp)
            inv = 1.0 / (1.0 + above + below * (1.0 - c))
            c = above * inv
            lower = below * inv
            v0 = r0 * inv + lower * v0
            v1 = r1 * inv + lower * v1
            v2 = r2 * inv + lower * v2
            l = lower * l
            for k, value in enumerate((v0, v1, v2, l, c)):
                V[k, yc, i] = value
            f0 = f0 + fr * v0
            f1 = f1 + fr * v1
            f2 = f2 + fr * v2
            fl = fl + fr * l
            fr = fr * c
            return (fuy_now, fuy_next, fuz_now, fuz_next, u_zn_next, u_zp_next,
                    c, v0, v1, v2, l, f0, f1, f2, fl, fr)

        u_low, u_mid = ld(0, 0), ld(0, 1)
        u_zn, u_zp = z_next(u_mid), z_prev(u_mid)
        zero = jnp.zeros((T, ROWS, LANES), jnp.float32)
        one = jnp.ones((T, ROWS, LANES), jnp.float32)
        state = (flux_uy(0), flux_uy(1), ld(3, 0) * z_diff(u_low), ld(3, 1) * (u_zn - u_zp), u_zn, u_zp,
                 zero, zero, zero, zero, one, zero, zero, zero, zero, one)
        state = lax.fori_loop(0, X, row, state)
        c, v0, v1, v2, l, f0, f1, f2, fl, fr = state[6:]
        for k, value in enumerate((f0, f1, f2, fl, fr, v0, v1, v2, l, c)):
            TP[yc, k] = value

    def p_copy(yc):
        return pltpu.make_async_remote_copy(
            src_ref=PS.at[yc], dst_ref=PR.at[yc],
            send_sem=p_send.at[yc], recv_sem=p_recv.at[yc],
            device_id=(gx + 1, gy), device_id_type=MESH,
        )

    def s_copy(yc):
        return pltpu.make_async_remote_copy(
            src_ref=SS.at[yc], dst_ref=SR.at[yc],
            send_sem=s_send.at[yc], recv_sem=s_recv.at[yc],
            device_id=(gx - 1, gy), device_id_type=MESH,
        )

    @pl.when(gx == 0)
    def _():
        PR[...] = jnp.zeros(PR.shape, jnp.float32)

    @pl.when(gx == nx - 1)
    def _():
        SR[...] = jnp.zeros(SR.shape, jnp.float32)

    def relate(yc, came, give, near, far):
        near0, near_own, near_other = near
        far0, far_own, far_other = far
        q = came[yc, 3]
        own = TP[yc, near_own]
        m = q / (1.0 - own * q)
        gain = TP[yc, far_own]
        for k in range(3):
            p = came[yc, k]
            give[yc, k] = TP[yc, far0 + k] + gain * (p + m * (TP[yc, near0 + k] + own * p))
        give[yc, 3] = TP[yc, far_other] + gain * m * TP[yc, near_other]

    def close(yc):
        t_p, q_p = SR[yc, 3], PS[yc, 3]
        t_s, q_s = PR[yc, 3], SS[yc, 3]
        high_inv = 1.0 / (1.0 - t_p * q_p)
        low_inv = 1.0 / (1.0 - t_s * q_s)
        for k in range(3):
            ends_out[yc, k] = (PR[yc, k] + t_s * SS[yc, k]) * low_inv
            ends_out[yc, 3 + k] = (SR[yc, k] + t_p * PS[yc, k]) * high_inv

    def pass_up(k, carry):
        @pl.when(has_x[0])
        def _():
            p_copy(k).wait_recv()
        relate(k, PR, PS, (0, 3, 4), (5, 8, 9))

        @pl.when(has_x[1])
        def _():
            p_copy(k).start()
        return carry

    def pass_down(k, carry):
        @pl.when(has_x[1])
        def _():
            s_copy(k).wait_recv()
        relate(k, SR, SS, (5, 9, 8), (0, 4, 3))

        @pl.when(has_x[0])
        def _():
            s_copy(k).start()
        return carry

    ends = min(2, chunks)

    def loop_inner(body):
        if chunks > 2:
            lax.fori_loop(1, chunks - 1, body, 0)

    def loop_outermost(body):
        lax.fori_loop(0, ends, lambda k, carry: body(k * (chunks - 1), carry), 0)

    low_half = gx < nx // 2

    def in_order(loop, low_body, high_body):
        @pl.when(low_half)
        def _():
            loop(low_body)

        @pl.when(jnp.logical_not(low_half))
        def _():
            loop(high_body)

    def compute_step(yc, carry):
        compute_chunk(yc)
        return carry

    loop_inner(compute_step)
    in_order(loop_inner, pass_up, pass_down)

    for s in (0, 1):
        @pl.when(has_y[s])
        def _():
            for f in range(FIELDS):
                y_copy(s, f).wait_send()
                y_copy(1 - s, f).wait_recv()

            def spread(f, carry):
                F[f, 1:X + 1, :, outer[s]:outer[s] + 1, :] = ER[s, f]
                return carry
            lax.fori_loop(0, FIELDS, spread, 0)
    for a in (0, 1):
        for b in (0, 1):
            @pl.when(jnp.logical_and(has_x[a], has_y[b]))
            def _():
                c_copy(a, b).wait_send()
                c_copy(1 - a, 1 - b).wait_recv()
                for f in (0, 1):
                    F[f, (X + 1) * a, :, outer[b]:outer[b] + 1, :] = CR[a, b, f]

    loop_outermost(compute_step)
    in_order(loop_outermost, pass_up, pass_down)
    in_order(loop_inner, pass_down, pass_up)
    in_order(loop_outermost, pass_down, pass_up)

    def close_step(yc, carry):
        close(yc)
        return carry

    lax.fori_loop(0, chunks, close_step, 0)

    for yc in range(chunks):
        @pl.when(has_x[1])
        def _():
            p_copy(yc).wait_send()

        @pl.when(has_x[0])
        def _():
            s_copy(yc).wait_send()


def substitute(V, ends, u_out, v_out, w_out, O, o_sem):
    _, chunks, X, T, _, _ = V.shape
    outputs = (u_out, v_out, w_out)

    def copy(k, yc):
        part = pl.ds(pl.multiple_of(yc * ROWS, ROWS), ROWS)
        return pltpu.make_async_copy(O.at[k, :, part, :], outputs[k].at[:, part, :], o_sem.at[k, yc])

    def chunk(yc, carry):
        low = [ends[yc, k] for k in range(3)]

        def row(n, now):
            i = X - 1 - n
            l, c = V[3, yc, i], V[4, yc, i]
            now = tuple(V[k, yc, i] + l * low[k] + c * now[k] for k in range(3))
            for k in range(3):
                for t in range(T):
                    O[k, i, pl.ds(pl.multiple_of(yc * ROWS, ROWS), ROWS), t * LANES:(t + 1) * LANES] = now[k][t]
            return now

        lax.fori_loop(0, X, row, tuple(ends[yc, 3 + k] for k in range(3)))
        for k in range(3):
            copy(k, yc).start()
        return carry

    lax.fori_loop(0, chunks, chunk, 0)
    for yc in range(chunks):
        for k in range(3):
            copy(k, yc).wait()


def per_device(nx, ny, u_velocity, v_velocity, w_velocity, viscosity, cell_width):
    X, Y, Z = u_velocity.shape
    T = Z // LANES
    chunks = Y // ROWS
    f32 = jnp.float32
    dma = pltpu.SemaphoreType.DMA
    in_hbm = pl.BlockSpec(memory_space=pltpu.HBM)
    in_vmem = pl.BlockSpec(memory_space=pltpu.VMEM)
    out = jax.ShapeDtypeStruct((X, Y, Z), f32)
    rows, ends = pl.pallas_call(
        functools.partial(kernel, nx, ny),
        out_shape=(
            pltpu.VMEM((5, chunks, X, T, ROWS, LANES), f32),
            pltpu.VMEM((chunks, 6, T, ROWS, LANES), f32),
        ),
        in_specs=[in_hbm] * 5,
        out_specs=(in_vmem,) * 2,
        scratch_shapes=[
            pltpu.VMEM((FIELDS, X + 2, T, Y + 2 * PAD, LANES), f32),
            pltpu.VMEM((X + 2, ROWS, LANES), f32),
            pltpu.VMEM((X, ROWS, LANES), f32),
            pltpu.VMEM((X, ROWS, LANES), f32),
            pltpu.VMEM((X, ROWS, LANES), f32),
            pltpu.VMEM((2, FIELDS, Y, Z), f32),
            pltpu.VMEM((2, FIELDS, X, T, 1, LANES), f32),
            pltpu.VMEM((2, FIELDS, X, T, 1, LANES), f32),
            pltpu.VMEM((2, 2, 2, T, 1, LANES), f32),
            pltpu.VMEM((chunks, 10, T, ROWS, LANES), f32),
            pltpu.VMEM((chunks, 4, T, ROWS, LANES), f32),
            pltpu.VMEM((chunks, 4, T, ROWS, LANES), f32),
            pltpu.VMEM((chunks, 4, T, ROWS, LANES), f32),
            pltpu.VMEM((chunks, 4, T, ROWS, LANES), f32),
            pltpu.SMEM((X,), f32),
            dma, dma((FIELDS, T)),
            dma((2, FIELDS)), dma((2, FIELDS)),
            dma((2, FIELDS)), dma((2, FIELDS)),
            dma((2, 2)), dma((2, 2)),
            dma((2,)), dma((2,)),
            dma((chunks,)), dma((chunks,)),
            dma((chunks,)), dma((chunks,)),
        ],
        compiler_params=pltpu.CompilerParams(
            collective_id=0, has_side_effects=True, vmem_limit_bytes=54 * 1024 * 1024
        ),
    )(u_velocity, v_velocity, w_velocity, viscosity, cell_width)
    return pl.pallas_call(
        substitute,
        out_shape=(out, out, out),
        in_specs=[in_vmem] * 2,
        out_specs=(in_hbm,) * 3,
        scratch_shapes=[pltpu.VMEM((3, X, Y, Z), f32), dma((3, chunks))],
        compiler_params=pltpu.CompilerParams(vmem_limit_bytes=16 * 1024 * 1024),
    )(rows, ends)


def solution(mesh):
    spec = P("gx", "gy", None)
    return jax.shard_map(
        functools.partial(per_device, mesh.shape["gx"], mesh.shape["gy"]),
        mesh=mesh,
        in_specs=(spec, spec, spec, spec, P("gx")),
        out_specs=(spec, spec, spec),
        check_vma=False,
    )
```

```python
import functools

import jax
import jax.numpy as jnp
from jax import lax
from jax.experimental import pallas as pl
from jax.experimental.pallas import tpu as pltpu
from jax.sharding import PartitionSpec as P

time_step = 0.0125
face_factor = 2.0

LANES = 128
ROWS = 8
PAD = 8
FIELDS = 4
MESH = pl.DeviceIdType.MESH


def kernel(
    nx, ny,
    u_ref, v_ref, w_ref, nu_ref, width_in,
    V, ends_out,
    F, wv, span_inv, below_c, above_c, XH, ES, ER, CR, TP, PR, PS, SR, SS, width_ref,
    width_sem, local_sem, x_send, x_recv, y_send, y_recv, c_send, c_recv, w_send, w_recv,
    p_send, p_recv, s_send, s_recv,
):
    X, Y, Z = u_ref.shape
    T = Z // LANES
    chunks = Y // ROWS
    gx = lax.axis_index("gx")
    gy = lax.axis_index("gy")
    has_x = (gx > 0, gx < nx - 1)
    has_y = (gy > 0, gy < ny - 1)
    inputs = (u_ref, v_ref, w_ref, nu_ref)

    def local_copies():
        return [
            pltpu.make_async_copy(
                inputs[f].at[:, :, t * LANES:(t + 1) * LANES],
                F.at[f, 1:X + 1, t, PAD:PAD + Y, :],
                local_sem.at[f, t],
            )
            for f in range(FIELDS) for t in range(T)
        ]

    width_copy = pltpu.make_async_copy(width_in, width_ref, width_sem)
    width_copy.start()
    for copy in local_copies():
        copy.start()

    barrier = pltpu.get_barrier_semaphore()
    partners = []
    for dx in (-1, 0, 1):
        for dy in (-1, 0, 1):
            if dx == 0 and dy == 0:
                continue
            ok = None
            if dx:
                ok = has_x[(dx + 1) // 2]
            if dy:
                oky = has_y[(dy + 1) // 2]
                ok = oky if ok is None else jnp.logical_and(ok, oky)
            partners.append((dx, dy, ok))
    for dx, dy, ok in partners:
        @pl.when(ok)
        def _():
            pl.semaphore_signal(barrier, inc=1, device_id=(gx + dx, gy + dy), device_id_type=MESH)
    near_x = has_x[0].astype(jnp.int32) + has_x[1].astype(jnp.int32)
    near_y = has_y[0].astype(jnp.int32) + has_y[1].astype(jnp.int32)
    pl.semaphore_wait(barrier, near_x + near_y + near_x * near_y)

    def x_copy(s, f):
        return pltpu.make_async_remote_copy(
            src_ref=inputs[f].at[(X - 1) * s],
            dst_ref=XH.at[1 - s, f],
            send_sem=x_send.at[s, f], recv_sem=x_recv.at[1 - s, f],
            device_id=(gx + 2 * s - 1, gy), device_id_type=MESH,
        )

    def w_copy(s):
        return pltpu.make_async_remote_copy(
            src_ref=wv.at[X if s else 1],
            dst_ref=wv.at[0 if s else X + 1],
            send_sem=w_send.at[s], recv_sem=w_recv.at[1 - s],
            device_id=(gx + 2 * s - 1, gy), device_id_type=MESH,
        )

    def y_copy(s, f):
        return pltpu.make_async_remote_copy(
            src_ref=ES.at[s, f], dst_ref=ER.at[1 - s, f],
            send_sem=y_send.at[s, f], recv_sem=y_recv.at[1 - s, f],
            device_id=(gx, gy + 2 * s - 1), device_id_type=MESH,
        )

    def c_copy(a, b):
        return pltpu.make_async_remote_copy(
            src_ref=ES.at[b, 0:2, (X - 1) * a], dst_ref=CR.at[1 - a, 1 - b],
            send_sem=c_send.at[a, b], recv_sem=c_recv.at[1 - a, 1 - b],
            device_id=(gx + 2 * a - 1, gy + 2 * b - 1), device_id_type=MESH,
        )

    for s in (0, 1):
        @pl.when(has_x[s])
        def _():
            for f in range(FIELDS):
                x_copy(s, f).start()

    width_copy.wait()
    for i in range(X):
        wv[i + 1] = jnp.full((ROWS, LANES), width_ref[i], jnp.float32)
    for s in (0, 1):
        @pl.when(has_x[s])
        def _():
            w_copy(s).start()

        @pl.when(jnp.logical_not(has_x[s]))
        def _():
            wv[(X + 1) * s] = jnp.zeros((ROWS, LANES), jnp.float32)

    edge = (PAD, PAD + Y - 1)
    outer = (PAD - 1, PAD + Y)
    arriving = local_copies()
    for f in range(FIELDS):
        for copy in arriving[f * T:(f + 1) * T]:
            copy.wait()
        for s in (0, 1):
            @pl.when(has_y[s])
            def _():
                ES[s, f] = F[f, 1:X + 1, :, edge[s]:edge[s] + 1, :]
                y_copy(s, f).start()
    for a in (0, 1):
        for b in (0, 1):
            @pl.when(jnp.logical_and(has_x[a], has_y[b]))
            def _():
                c_copy(a, b).start()

    for s in (0, 1):
        @pl.when(jnp.logical_not(has_y[s]))
        def _():
            def fill(f, carry):
                F[f, :, :, outer[s]:outer[s] + 1, :] = jnp.zeros((X + 2, T, 1, LANES), jnp.float32)
                return carry
            lax.fori_loop(0, FIELDS, fill, 0)

        @pl.when(jnp.logical_not(has_x[s]))
        def _():
            def fill(f, carry):
                F[f, (X + 1) * s] = jnp.zeros((T, Y + 2 * PAD, LANES), jnp.float32)
                return carry
            lax.fori_loop(0, FIELDS, fill, 0)

    for s in (0, 1):
        @pl.when(has_x[s])
        def _():
            w_copy(s).wait_send()
            w_copy(1 - s).wait_recv()
            for f in range(FIELDS):
                x_copy(s, f).wait_send()
                x_copy(1 - s, f).wait_recv()

            def spread(f, carry):
                for t in range(T):
                    F[f, (X + 1) * s, t, PAD:PAD + Y, :] = XH[s, f, :, t * LANES:(t + 1) * LANES]
                return carry
            lax.fori_loop(0, FIELDS, spread, 0)

    for i in range(X):
        low, mid, high = wv[i], wv[i + 1], wv[i + 2]
        span_inv[i] = 1.0 / (0.5 * low + mid + 0.5 * high)
        below_c[i] = time_step / (mid * (low + mid))
        above_c[i] = time_step / (mid * (mid + high))

    lane = lax.broadcasted_iota(jnp.int32, (T, ROWS, LANES), 2)
    first_lane = lane == 0
    last_lane = lane == LANES - 1
    zero_tile = jnp.zeros((1, ROWS, LANES), jnp.float32)

    def z_next(a):
        r = pltpu.roll(a, LANES - 1, 2)
        after = jnp.concatenate([r[1:], zero_tile], axis=0)
        return jnp.where(last_lane, after, r)

    def z_prev(a):
        r = pltpu.roll(a, 1, 2)
        before = jnp.concatenate([zero_tile, r[:-1]], axis=0)
        return jnp.where(first_lane, before, r)

    def z_diff(a):
        return z_next(a) - z_prev(a)

    def compute_chunk(yc):
        base = PAD + yc * ROWS

        def ld(f, i, dy=0):
            return F[f, i, :, pl.ds(base + dy, ROWS), :]

        def flux_uy(i):
            return ld(3, i) * (ld(0, i, 1) - ld(0, i, -1))

        def row(i, state):
            (fuy_prev, fuy_now, fuz_prev, fuz_now, u_zn, u_zp,
             c, v0, v1, v2, l, f0, f1, f2, fl, fr) = state
            inv_s = span_inv[i][None]
            nu0, nu_xp, nu_xm = ld(3, i + 1), ld(3, i + 2), ld(3, i)
            nu_yp, nu_ym = ld(3, i + 1, 1), ld(3, i + 1, -1)
            u_next_row = ld(0, i + 2)
            u_zn_next, u_zp_next = z_next(u_next_row), z_prev(u_next_row)
            fuy_next = flux_uy(i + 2)
            fuz_next = nu_xp * (u_zn_next - u_zp_next)

            face_yp, face_ym = nu0 + nu_yp, nu0 + nu_ym
            face_zp, face_zm = nu0 + z_next(nu0), nu0 + z_prev(nu0)
            face_sum = (face_yp + face_ym) + (face_zp + face_zm)
            mid = [ld(f, i + 1) for f in range(3)]
            u_scaled = mid[0] * inv_s

            x_dw = ld(2, i + 2) - ld(2, i)
            v_yp, v_ym = ld(1, i + 1, 1), ld(1, i + 1, -1)
            w_yp, w_ym = ld(2, i + 1, 1), ld(2, i + 1, -1)
            cross_u = inv_s * (
                nu_yp * (ld(1, i + 2, 1) - ld(1, i, 1))
                - nu_ym * (ld(1, i + 2, -1) - ld(1, i, -1))
                + z_diff(nu0 * x_dw)
            )
            cross_v = inv_s * (fuy_next - fuy_prev) + z_diff(nu0 * (w_yp - w_ym))
            cross_w = inv_s * (fuz_next - fuz_prev) + (nu_yp * z_diff(v_yp) - nu_ym * z_diff(v_ym))

            def side(f, cross, yp, ym, zn, zp, x_d):
                q = mid[f]
                advect = u_scaled * x_d + mid[1] * (yp - ym) + mid[2] * (zn - zp)
                spread = (face_yp * yp + face_ym * ym) + (face_zp * zn + face_zm * zp) - face_sum * q
                return q + time_step * (face_factor * spread + (cross - advect))

            r0 = side(0, cross_u, ld(0, i + 1, 1), ld(0, i + 1, -1), u_zn, u_zp, u_next_row - ld(0, i))
            r1 = side(1, cross_v, v_yp, v_ym, z_next(mid[1]), z_prev(mid[1]), ld(1, i + 2) - ld(1, i))
            r2 = side(2, cross_w, w_yp, w_ym, z_next(mid[2]), z_prev(mid[2]), x_dw)

            below = below_c[i][None] * (nu0 + nu_xm)
            above = above_c[i][None] * (nu0 + nu_xp)
            inv = 1.0 / (1.0 + above + below * (1.0 - c))
            c = above * inv
            lower = below * inv
            v0 = r0 * inv + lower * v0
            v1 = r1 * inv + lower * v1
            v2 = r2 * inv + lower * v2
            l = lower * l
            for k, value in enumerate((v0, v1, v2, l, c)):
                V[k, yc, i] = value
            f0 = f0 + fr * v0
            f1 = f1 + fr * v1
            f2 = f2 + fr * v2
            fl = fl + fr * l
            fr = fr * c
            return (fuy_now, fuy_next, fuz_now, fuz_next, u_zn_next, u_zp_next,
                    c, v0, v1, v2, l, f0, f1, f2, fl, fr)

        u_low, u_mid = ld(0, 0), ld(0, 1)
        u_zn, u_zp = z_next(u_mid), z_prev(u_mid)
        zero = jnp.zeros((T, ROWS, LANES), jnp.float32)
        one = jnp.ones((T, ROWS, LANES), jnp.float32)
        state = (flux_uy(0), flux_uy(1), ld(3, 0) * z_diff(u_low), ld(3, 1) * (u_zn - u_zp), u_zn, u_zp,
                 zero, zero, zero, zero, one, zero, zero, zero, zero, one)
        state = lax.fori_loop(0, X, row, state, unroll=8)
        c, v0, v1, v2, l, f0, f1, f2, fl, fr = state[6:]
        for k, value in enumerate((f0, f1, f2, fl, fr, v0, v1, v2, l, c)):
            TP[yc, k] = value

    def p_copy(yc):
        return pltpu.make_async_remote_copy(
            src_ref=PS.at[yc], dst_ref=PR.at[yc],
            send_sem=p_send.at[yc], recv_sem=p_recv.at[yc],
            device_id=(gx + 1, gy), device_id_type=MESH,
        )

    def s_copy(yc):
        return pltpu.make_async_remote_copy(
            src_ref=SS.at[yc], dst_ref=SR.at[yc],
            send_sem=s_send.at[yc], recv_sem=s_recv.at[yc],
            device_id=(gx - 1, gy), device_id_type=MESH,
        )

    @pl.when(gx == 0)
    def _():
        PR[...] = jnp.zeros(PR.shape, jnp.float32)

    @pl.when(gx == nx - 1)
    def _():
        SR[...] = jnp.zeros(SR.shape, jnp.float32)

    def relate(yc, came, give, near, far):
        near0, near_own, near_other = near
        far0, far_own, far_other = far
        q = came[yc, 3]
        own = TP[yc, near_own]
        m = q / (1.0 - own * q)
        gain = TP[yc, far_own]
        for k in range(3):
            p = came[yc, k]
            give[yc, k] = TP[yc, far0 + k] + gain * (p + m * (TP[yc, near0 + k] + own * p))
        give[yc, 3] = TP[yc, far_other] + gain * m * TP[yc, near_other]

    def close(yc):
        t_p, q_p = SR[yc, 3], PS[yc, 3]
        t_s, q_s = PR[yc, 3], SS[yc, 3]
        high_inv = 1.0 / (1.0 - t_p * q_p)
        low_inv = 1.0 / (1.0 - t_s * q_s)
        for k in range(3):
            ends_out[yc, k] = (PR[yc, k] + t_s * SS[yc, k]) * low_inv
            ends_out[yc, 3 + k] = (SR[yc, k] + t_p * PS[yc, k]) * high_inv

    def pass_up(k, carry):
        @pl.when(has_x[0])
        def _():
            p_copy(k).wait_recv()
        relate(k, PR, PS, (0, 3, 4), (5, 8, 9))

        @pl.when(has_x[1])
        def _():
            p_copy(k).start()
        return carry

    def pass_down(k, carry):
        @pl.when(has_x[1])
        def _():
            s_copy(k).wait_recv()
        relate(k, SR, SS, (5, 9, 8), (0, 4, 3))

        @pl.when(has_x[0])
        def _():
            s_copy(k).start()
        return carry

    ends = min(2, chunks)

    def loop_inner(body):
        if chunks > 2:
            lax.fori_loop(1, chunks - 1, body, 0)

    def loop_outermost(body):
        lax.fori_loop(0, ends, lambda k, carry: body(k * (chunks - 1), carry), 0)

    low_half = gx < nx // 2

    def in_order(loop, low_body, high_body):
        @pl.when(low_half)
        def _():
            loop(low_body)

        @pl.when(jnp.logical_not(low_half))
        def _():
            loop(high_body)

    def compute_step(yc, carry):
        compute_chunk(yc)
        return carry

    def compute_and_pass(yc, carry):
        compute_chunk(yc)

        @pl.when(low_half)
        def _():
            pass_up(yc, 0)

        @pl.when(jnp.logical_not(low_half))
        def _():
            pass_down(yc, 0)
        return carry

    loop_inner(compute_step)
    in_order(loop_inner, pass_up, pass_down)

    for s in (0, 1):
        @pl.when(has_y[s])
        def _():
            for f in range(FIELDS):
                y_copy(s, f).wait_send()
                y_copy(1 - s, f).wait_recv()

            def spread(f, carry):
                F[f, 1:X + 1, :, outer[s]:outer[s] + 1, :] = ER[s, f]
                return carry
            lax.fori_loop(0, FIELDS, spread, 0)
    for a in (0, 1):
        for b in (0, 1):
            @pl.when(jnp.logical_and(has_x[a], has_y[b]))
            def _():
                c_copy(a, b).wait_send()
                c_copy(1 - a, 1 - b).wait_recv()
                for f in (0, 1):
                    F[f, (X + 1) * a, :, outer[b]:outer[b] + 1, :] = CR[a, b, f]

    loop_outermost(compute_and_pass)
    in_order(loop_inner, pass_down, pass_up)
    in_order(loop_outermost, pass_down, pass_up)

    def close_step(yc, carry):
        close(yc)
        return carry

    lax.fori_loop(0, chunks, close_step, 0)

    for yc in range(chunks):
        @pl.when(has_x[1])
        def _():
            p_copy(yc).wait_send()

        @pl.when(has_x[0])
        def _():
            s_copy(yc).wait_send()


def substitute(V, ends, u_out, v_out, w_out, O, o_sem):
    _, chunks, X, T, _, _ = V.shape
    outputs = (u_out, v_out, w_out)

    def copy(k, yc):
        part = pl.ds(pl.multiple_of(yc * ROWS, ROWS), ROWS)
        return pltpu.make_async_copy(O.at[k, :, part, :], outputs[k].at[:, part, :], o_sem.at[k, yc])

    def chunk(yc, carry):
        low = [ends[yc, k] for k in range(3)]

        def row(n, now):
            i = X - 1 - n
            l, c = V[3, yc, i], V[4, yc, i]
            now = tuple(V[k, yc, i] + l * low[k] + c * now[k] for k in range(3))
            for k in range(3):
                for t in range(T):
                    O[k, i, pl.ds(pl.multiple_of(yc * ROWS, ROWS), ROWS), t * LANES:(t + 1) * LANES] = now[k][t]
            return now

        lax.fori_loop(0, X, row, tuple(ends[yc, 3 + k] for k in range(3)), unroll=4)
        for k in range(3):
            copy(k, yc).start()
        return carry

    lax.fori_loop(0, chunks, chunk, 0)
    for yc in range(chunks):
        for k in range(3):
            copy(k, yc).wait()


def per_device(nx, ny, u_velocity, v_velocity, w_velocity, viscosity, cell_width):
    X, Y, Z = u_velocity.shape
    T = Z // LANES
    chunks = Y // ROWS
    f32 = jnp.float32
    dma = pltpu.SemaphoreType.DMA
    in_hbm = pl.BlockSpec(memory_space=pltpu.HBM)
    in_vmem = pl.BlockSpec(memory_space=pltpu.VMEM)
    out = jax.ShapeDtypeStruct((X, Y, Z), f32)
    rows, ends = pl.pallas_call(
        functools.partial(kernel, nx, ny),
        out_shape=(
            pltpu.VMEM((5, chunks, X, T, ROWS, LANES), f32),
            pltpu.VMEM((chunks, 6, T, ROWS, LANES), f32),
        ),
        in_specs=[in_hbm] * 5,
        out_specs=(in_vmem,) * 2,
        scratch_shapes=[
            pltpu.VMEM((FIELDS, X + 2, T, Y + 2 * PAD, LANES), f32),
            pltpu.VMEM((X + 2, ROWS, LANES), f32),
            pltpu.VMEM((X, ROWS, LANES), f32),
            pltpu.VMEM((X, ROWS, LANES), f32),
            pltpu.VMEM((X, ROWS, LANES), f32),
            pltpu.VMEM((2, FIELDS, Y, Z), f32),
            pltpu.VMEM((2, FIELDS, X, T, 1, LANES), f32),
            pltpu.VMEM((2, FIELDS, X, T, 1, LANES), f32),
            pltpu.VMEM((2, 2, 2, T, 1, LANES), f32),
            pltpu.VMEM((chunks, 10, T, ROWS, LANES), f32),
            pltpu.VMEM((chunks, 4, T, ROWS, LANES), f32),
            pltpu.VMEM((chunks, 4, T, ROWS, LANES), f32),
            pltpu.VMEM((chunks, 4, T, ROWS, LANES), f32),
            pltpu.VMEM((chunks, 4, T, ROWS, LANES), f32),
            pltpu.SMEM((X,), f32),
            dma, dma((FIELDS, T)),
            dma((2, FIELDS)), dma((2, FIELDS)),
            dma((2, FIELDS)), dma((2, FIELDS)),
            dma((2, 2)), dma((2, 2)),
            dma((2,)), dma((2,)),
            dma((chunks,)), dma((chunks,)),
            dma((chunks,)), dma((chunks,)),
        ],
        compiler_params=pltpu.CompilerParams(
            collective_id=0, has_side_effects=True, vmem_limit_bytes=54 * 1024 * 1024
        ),
    )(u_velocity, v_velocity, w_velocity, viscosity, cell_width)
    return pl.pallas_call(
        substitute,
        out_shape=(out, out, out),
        in_specs=[in_vmem] * 2,
        out_specs=(in_hbm,) * 3,
        scratch_shapes=[pltpu.VMEM((3, X, Y, Z), f32), dma((3, chunks))],
        compiler_params=pltpu.CompilerParams(vmem_limit_bytes=16 * 1024 * 1024),
    )(rows, ends)


def solution(mesh):
    spec = P("gx", "gy", None)
    return jax.shard_map(
        functools.partial(per_device, mesh.shape["gx"], mesh.shape["gy"]),
        mesh=mesh,
        in_specs=(spec, spec, spec, spec, P("gx")),
        out_specs=(spec, spec, spec),
        check_vma=False,
    )
```

```python
import functools

import jax
import jax.numpy as jnp
from jax import lax
from jax.experimental import pallas as pl
from jax.experimental.pallas import tpu as pltpu
from jax.sharding import PartitionSpec as P

time_step = 0.0125
face_factor = 2.0

LANES = 128
ROWS = 8
PAD = 8
FIELDS = 4
MESH = pl.DeviceIdType.MESH


def kernel(
    nx, ny,
    u_ref, v_ref, w_ref, nu_ref, width_in,
    V, ends_out,
    F, wv, span_inv, below_c, above_c, XH, ES, ER, CR, TP, PR, PS, SR, SS, width_ref,
    width_sem, local_sem, x_send, x_recv, y_send, y_recv, c_send, c_recv, w_send, w_recv,
    p_send, p_recv, s_send, s_recv,
):
    X, Y, Z = u_ref.shape
    T = Z // LANES
    chunks = Y // ROWS
    gx = lax.axis_index("gx")
    gy = lax.axis_index("gy")
    has_x = (gx > 0, gx < nx - 1)
    has_y = (gy > 0, gy < ny - 1)
    inputs = (u_ref, v_ref, w_ref, nu_ref)

    def local_copies():
        return [
            pltpu.make_async_copy(
                inputs[f].at[:, :, t * LANES:(t + 1) * LANES],
                F.at[f, 1:X + 1, t, PAD:PAD + Y, :],
                local_sem.at[f, t],
            )
            for f in range(FIELDS) for t in range(T)
        ]

    width_copy = pltpu.make_async_copy(width_in, width_ref, width_sem)
    width_copy.start()
    for copy in local_copies():
        copy.start()

    barrier = pltpu.get_barrier_semaphore()
    partners = []
    for dx in (-1, 0, 1):
        for dy in (-1, 0, 1):
            if dx == 0 and dy == 0:
                continue
            ok = None
            if dx:
                ok = has_x[(dx + 1) // 2]
            if dy:
                oky = has_y[(dy + 1) // 2]
                ok = oky if ok is None else jnp.logical_and(ok, oky)
            partners.append((dx, dy, ok))
    for dx, dy, ok in partners:
        @pl.when(ok)
        def _():
            pl.semaphore_signal(barrier, inc=1, device_id=(gx + dx, gy + dy), device_id_type=MESH)
    near_x = has_x[0].astype(jnp.int32) + has_x[1].astype(jnp.int32)
    near_y = has_y[0].astype(jnp.int32) + has_y[1].astype(jnp.int32)
    pl.semaphore_wait(barrier, near_x + near_y + near_x * near_y)

    def x_copy(s, f):
        return pltpu.make_async_remote_copy(
            src_ref=inputs[f].at[(X - 1) * s],
            dst_ref=XH.at[1 - s, f],
            send_sem=x_send.at[s, f], recv_sem=x_recv.at[1 - s, f],
            device_id=(gx + 2 * s - 1, gy), device_id_type=MESH,
        )

    def w_copy(s):
        return pltpu.make_async_remote_copy(
            src_ref=wv.at[X if s else 1],
            dst_ref=wv.at[0 if s else X + 1],
            send_sem=w_send.at[s], recv_sem=w_recv.at[1 - s],
            device_id=(gx + 2 * s - 1, gy), device_id_type=MESH,
        )

    def y_copy(s, f):
        return pltpu.make_async_remote_copy(
            src_ref=ES.at[s, f], dst_ref=ER.at[1 - s, f],
            send_sem=y_send.at[s, f], recv_sem=y_recv.at[1 - s, f],
            device_id=(gx, gy + 2 * s - 1), device_id_type=MESH,
        )

    def c_copy(a, b):
        return pltpu.make_async_remote_copy(
            src_ref=ES.at[b, 0:2, (X - 1) * a], dst_ref=CR.at[1 - a, 1 - b],
            send_sem=c_send.at[a, b], recv_sem=c_recv.at[1 - a, 1 - b],
            device_id=(gx + 2 * a - 1, gy + 2 * b - 1), device_id_type=MESH,
        )

    for s in (0, 1):
        @pl.when(has_x[s])
        def _():
            for f in range(FIELDS):
                x_copy(s, f).start()

    width_copy.wait()
    for i in range(X):
        wv[i + 1] = jnp.full((ROWS, LANES), width_ref[i], jnp.float32)
    for s in (0, 1):
        @pl.when(has_x[s])
        def _():
            w_copy(s).start()

        @pl.when(jnp.logical_not(has_x[s]))
        def _():
            wv[(X + 1) * s] = jnp.zeros((ROWS, LANES), jnp.float32)

    edge = (PAD, PAD + Y - 1)
    outer = (PAD - 1, PAD + Y)
    arriving = local_copies()
    for f in range(FIELDS):
        for copy in arriving[f * T:(f + 1) * T]:
            copy.wait()
        for s in (0, 1):
            @pl.when(has_y[s])
            def _():
                ES[s, f] = F[f, 1:X + 1, :, edge[s]:edge[s] + 1, :]
                y_copy(s, f).start()
    for a in (0, 1):
        for b in (0, 1):
            @pl.when(jnp.logical_and(has_x[a], has_y[b]))
            def _():
                c_copy(a, b).start()

    for s in (0, 1):
        @pl.when(jnp.logical_not(has_y[s]))
        def _():
            def fill(f, carry):
                F[f, :, :, outer[s]:outer[s] + 1, :] = jnp.zeros((X + 2, T, 1, LANES), jnp.float32)
                return carry
            lax.fori_loop(0, FIELDS, fill, 0)

        @pl.when(jnp.logical_not(has_x[s]))
        def _():
            def fill(f, carry):
                F[f, (X + 1) * s] = jnp.zeros((T, Y + 2 * PAD, LANES), jnp.float32)
                return carry
            lax.fori_loop(0, FIELDS, fill, 0)

    for s in (0, 1):
        @pl.when(has_x[s])
        def _():
            w_copy(s).wait_send()
            w_copy(1 - s).wait_recv()
            for f in range(FIELDS):
                x_copy(s, f).wait_send()
                x_copy(1 - s, f).wait_recv()

            def spread(f, carry):
                for t in range(T):
                    F[f, (X + 1) * s, t, PAD:PAD + Y, :] = XH[s, f, :, t * LANES:(t + 1) * LANES]
                return carry
            lax.fori_loop(0, FIELDS, spread, 0)

    for i in range(X):
        low, mid, high = wv[i], wv[i + 1], wv[i + 2]
        span_inv[i] = 1.0 / (0.5 * low + mid + 0.5 * high)
        below_c[i] = time_step / (mid * (low + mid))
        above_c[i] = time_step / (mid * (mid + high))

    lane = lax.broadcasted_iota(jnp.int32, (T, ROWS, LANES), 2)
    first_lane = lane == 0
    last_lane = lane == LANES - 1
    zero_tile = jnp.zeros((1, ROWS, LANES), jnp.float32)

    def z_next(a):
        r = pltpu.roll(a, LANES - 1, 2)
        after = jnp.concatenate([r[1:], zero_tile], axis=0)
        return jnp.where(last_lane, after, r)

    def z_prev(a):
        r = pltpu.roll(a, 1, 2)
        before = jnp.concatenate([zero_tile, r[:-1]], axis=0)
        return jnp.where(first_lane, before, r)

    def z_diff(a):
        return z_next(a) - z_prev(a)

    def compute_chunk(yc):
        base = PAD + yc * ROWS

        def ld(f, i, dy=0):
            return F[f, i, :, pl.ds(base + dy, ROWS), :]

        def flux_uy(i):
            return ld(3, i) * (ld(0, i, 1) - ld(0, i, -1))

        def row(i, state):
            (fuy_prev, fuy_now, fuz_prev, fuz_now, u_zn, u_zp,
             c, v0, v1, v2, l, f0, f1, f2, fl, fr) = state
            inv_s = span_inv[i][None]
            nu0, nu_xp, nu_xm = ld(3, i + 1), ld(3, i + 2), ld(3, i)
            nu_yp, nu_ym = ld(3, i + 1, 1), ld(3, i + 1, -1)
            u_next_row = ld(0, i + 2)
            u_zn_next, u_zp_next = z_next(u_next_row), z_prev(u_next_row)
            fuy_next = flux_uy(i + 2)
            fuz_next = nu_xp * (u_zn_next - u_zp_next)

            face_yp, face_ym = nu0 + nu_yp, nu0 + nu_ym
            face_zp, face_zm = nu0 + z_next(nu0), nu0 + z_prev(nu0)
            face_sum = (face_yp + face_ym) + (face_zp + face_zm)
            mid = [ld(f, i + 1) for f in range(3)]
            u_scaled = mid[0] * inv_s

            x_dw = ld(2, i + 2) - ld(2, i)
            v_yp, v_ym = ld(1, i + 1, 1), ld(1, i + 1, -1)
            w_yp, w_ym = ld(2, i + 1, 1), ld(2, i + 1, -1)
            cross_u = inv_s * (
                nu_yp * (ld(1, i + 2, 1) - ld(1, i, 1))
                - nu_ym * (ld(1, i + 2, -1) - ld(1, i, -1))
                + z_diff(nu0 * x_dw)
            )
            cross_v = inv_s * (fuy_next - fuy_prev) + z_diff(nu0 * (w_yp - w_ym))
            cross_w = inv_s * (fuz_next - fuz_prev) + (nu_yp * z_diff(v_yp) - nu_ym * z_diff(v_ym))

            def side(f, cross, yp, ym, zn, zp, x_d):
                q = mid[f]
                advect = u_scaled * x_d + mid[1] * (yp - ym) + mid[2] * (zn - zp)
                spread = (face_yp * yp + face_ym * ym) + (face_zp * zn + face_zm * zp) - face_sum * q
                return q + time_step * (face_factor * spread + (cross - advect))

            r0 = side(0, cross_u, ld(0, i + 1, 1), ld(0, i + 1, -1), u_zn, u_zp, u_next_row - ld(0, i))
            r1 = side(1, cross_v, v_yp, v_ym, z_next(mid[1]), z_prev(mid[1]), ld(1, i + 2) - ld(1, i))
            r2 = side(2, cross_w, w_yp, w_ym, z_next(mid[2]), z_prev(mid[2]), x_dw)

            below = below_c[i][None] * (nu0 + nu_xm)
            above = above_c[i][None] * (nu0 + nu_xp)
            inv = 1.0 / (1.0 + above + below * (1.0 - c))
            c = above * inv
            lower = below * inv
            v0 = r0 * inv + lower * v0
            v1 = r1 * inv + lower * v1
            v2 = r2 * inv + lower * v2
            l = lower * l
            for k, value in enumerate((v0, v1, v2, l, c)):
                V[k, yc, i] = value
            f0 = f0 + fr * v0
            f1 = f1 + fr * v1
            f2 = f2 + fr * v2
            fl = fl + fr * l
            fr = fr * c
            return (fuy_now, fuy_next, fuz_now, fuz_next, u_zn_next, u_zp_next,
                    c, v0, v1, v2, l, f0, f1, f2, fl, fr)

        u_low, u_mid = ld(0, 0), ld(0, 1)
        u_zn, u_zp = z_next(u_mid), z_prev(u_mid)
        zero = jnp.zeros((T, ROWS, LANES), jnp.float32)
        one = jnp.ones((T, ROWS, LANES), jnp.float32)
        state = (flux_uy(0), flux_uy(1), ld(3, 0) * z_diff(u_low), ld(3, 1) * (u_zn - u_zp), u_zn, u_zp,
                 zero, zero, zero, zero, one, zero, zero, zero, zero, one)
        state = lax.fori_loop(0, X, row, state, unroll=True)
        c, v0, v1, v2, l, f0, f1, f2, fl, fr = state[6:]
        for k, value in enumerate((f0, f1, f2, fl, fr, v0, v1, v2, l, c)):
            TP[yc, k] = value

    def p_copy(yc):
        return pltpu.make_async_remote_copy(
            src_ref=PS.at[yc], dst_ref=PR.at[yc],
            send_sem=p_send.at[yc], recv_sem=p_recv.at[yc],
            device_id=(gx + 1, gy), device_id_type=MESH,
        )

    def s_copy(yc):
        return pltpu.make_async_remote_copy(
            src_ref=SS.at[yc], dst_ref=SR.at[yc],
            send_sem=s_send.at[yc], recv_sem=s_recv.at[yc],
            device_id=(gx - 1, gy), device_id_type=MESH,
        )

    @pl.when(gx == 0)
    def _():
        PR[...] = jnp.zeros(PR.shape, jnp.float32)

    @pl.when(gx == nx - 1)
    def _():
        SR[...] = jnp.zeros(SR.shape, jnp.float32)

    def relate(yc, came, give, near, far):
        near0, near_own, near_other = near
        far0, far_own, far_other = far
        q = came[yc, 3]
        own = TP[yc, near_own]
        m = q / (1.0 - own * q)
        gain = TP[yc, far_own]
        for k in range(3):
            p = came[yc, k]
            give[yc, k] = TP[yc, far0 + k] + gain * (p + m * (TP[yc, near0 + k] + own * p))
        give[yc, 3] = TP[yc, far_other] + gain * m * TP[yc, near_other]

    def close(yc):
        t_p, q_p = SR[yc, 3], PS[yc, 3]
        t_s, q_s = PR[yc, 3], SS[yc, 3]
        high_inv = 1.0 / (1.0 - t_p * q_p)
        low_inv = 1.0 / (1.0 - t_s * q_s)
        for k in range(3):
            ends_out[yc, k] = (PR[yc, k] + t_s * SS[yc, k]) * low_inv
            ends_out[yc, 3 + k] = (SR[yc, k] + t_p * PS[yc, k]) * high_inv

    def pass_up(k, carry):
        @pl.when(has_x[0])
        def _():
            p_copy(k).wait_recv()
        relate(k, PR, PS, (0, 3, 4), (5, 8, 9))

        @pl.when(has_x[1])
        def _():
            p_copy(k).start()
        return carry

    def pass_down(k, carry):
        @pl.when(has_x[1])
        def _():
            s_copy(k).wait_recv()
        relate(k, SR, SS, (5, 9, 8), (0, 4, 3))

        @pl.when(has_x[0])
        def _():
            s_copy(k).start()
        return carry

    ends = min(2, chunks)

    def loop_inner(body):
        if chunks > 2:
            lax.fori_loop(1, chunks - 1, body, 0)

    def loop_outermost(body):
        lax.fori_loop(0, ends, lambda k, carry: body(k * (chunks - 1), carry), 0)

    low_half = gx < nx // 2

    def in_order(loop, low_body, high_body):
        @pl.when(low_half)
        def _():
            loop(low_body)

        @pl.when(jnp.logical_not(low_half))
        def _():
            loop(high_body)

    def compute_step(yc, carry):
        compute_chunk(yc)
        return carry

    def compute_and_pass(yc, carry):
        compute_chunk(yc)

        @pl.when(low_half)
        def _():
            pass_up(yc, 0)

        @pl.when(jnp.logical_not(low_half))
        def _():
            pass_down(yc, 0)
        return carry

    loop_inner(compute_step)
    in_order(loop_inner, pass_up, pass_down)

    for s in (0, 1):
        @pl.when(has_y[s])
        def _():
            for f in range(FIELDS):
                y_copy(s, f).wait_send()
                y_copy(1 - s, f).wait_recv()

            def spread(f, carry):
                F[f, 1:X + 1, :, outer[s]:outer[s] + 1, :] = ER[s, f]
                return carry
            lax.fori_loop(0, FIELDS, spread, 0)
    for a in (0, 1):
        for b in (0, 1):
            @pl.when(jnp.logical_and(has_x[a], has_y[b]))
            def _():
                c_copy(a, b).wait_send()
                c_copy(1 - a, 1 - b).wait_recv()
                for f in (0, 1):
                    F[f, (X + 1) * a, :, outer[b]:outer[b] + 1, :] = CR[a, b, f]

    loop_outermost(compute_and_pass)
    in_order(loop_inner, pass_down, pass_up)
    in_order(loop_outermost, pass_down, pass_up)

    def close_step(yc, carry):
        close(yc)
        return carry

    lax.fori_loop(0, chunks, close_step, 0)

    for yc in range(chunks):
        @pl.when(has_x[1])
        def _():
            p_copy(yc).wait_send()

        @pl.when(has_x[0])
        def _():
            s_copy(yc).wait_send()


def substitute(V, ends, u_out, v_out, w_out, O, o_sem):
    _, chunks, X, T, _, _ = V.shape
    outputs = (u_out, v_out, w_out)

    def copy(k, yc):
        part = pl.ds(pl.multiple_of(yc * ROWS, ROWS), ROWS)
        return pltpu.make_async_copy(O.at[k, :, part, :], outputs[k].at[:, part, :], o_sem.at[k, yc])

    def chunk(yc, carry):
        low = [ends[yc, k] for k in range(3)]

        def row(n, now):
            i = X - 1 - n
            l, c = V[3, yc, i], V[4, yc, i]
            now = tuple(V[k, yc, i] + l * low[k] + c * now[k] for k in range(3))
            for k in range(3):
                for t in range(T):
                    O[k, i, pl.ds(pl.multiple_of(yc * ROWS, ROWS), ROWS), t * LANES:(t + 1) * LANES] = now[k][t]
            return now

        lax.fori_loop(0, X, row, tuple(ends[yc, 3 + k] for k in range(3)), unroll=4)
        for k in range(3):
            copy(k, yc).start()
        return carry

    lax.fori_loop(0, chunks, chunk, 0)
    for yc in range(chunks):
        for k in range(3):
            copy(k, yc).wait()


def per_device(nx, ny, u_velocity, v_velocity, w_velocity, viscosity, cell_width):
    X, Y, Z = u_velocity.shape
    T = Z // LANES
    chunks = Y // ROWS
    f32 = jnp.float32
    dma = pltpu.SemaphoreType.DMA
    in_hbm = pl.BlockSpec(memory_space=pltpu.HBM)
    in_vmem = pl.BlockSpec(memory_space=pltpu.VMEM)
    out = jax.ShapeDtypeStruct((X, Y, Z), f32)
    rows, ends = pl.pallas_call(
        functools.partial(kernel, nx, ny),
        out_shape=(
            pltpu.VMEM((5, chunks, X, T, ROWS, LANES), f32),
            pltpu.VMEM((chunks, 6, T, ROWS, LANES), f32),
        ),
        in_specs=[in_hbm] * 5,
        out_specs=(in_vmem,) * 2,
        scratch_shapes=[
            pltpu.VMEM((FIELDS, X + 2, T, Y + 2 * PAD, LANES), f32),
            pltpu.VMEM((X + 2, ROWS, LANES), f32),
            pltpu.VMEM((X, ROWS, LANES), f32),
            pltpu.VMEM((X, ROWS, LANES), f32),
            pltpu.VMEM((X, ROWS, LANES), f32),
            pltpu.VMEM((2, FIELDS, Y, Z), f32),
            pltpu.VMEM((2, FIELDS, X, T, 1, LANES), f32),
            pltpu.VMEM((2, FIELDS, X, T, 1, LANES), f32),
            pltpu.VMEM((2, 2, 2, T, 1, LANES), f32),
            pltpu.VMEM((chunks, 10, T, ROWS, LANES), f32),
            pltpu.VMEM((chunks, 4, T, ROWS, LANES), f32),
            pltpu.VMEM((chunks, 4, T, ROWS, LANES), f32),
            pltpu.VMEM((chunks, 4, T, ROWS, LANES), f32),
            pltpu.VMEM((chunks, 4, T, ROWS, LANES), f32),
            pltpu.SMEM((X,), f32),
            dma, dma((FIELDS, T)),
            dma((2, FIELDS)), dma((2, FIELDS)),
            dma((2, FIELDS)), dma((2, FIELDS)),
            dma((2, 2)), dma((2, 2)),
            dma((2,)), dma((2,)),
            dma((chunks,)), dma((chunks,)),
            dma((chunks,)), dma((chunks,)),
        ],
        compiler_params=pltpu.CompilerParams(
            collective_id=0, has_side_effects=True, vmem_limit_bytes=54 * 1024 * 1024
        ),
    )(u_velocity, v_velocity, w_velocity, viscosity, cell_width)
    return pl.pallas_call(
        substitute,
        out_shape=(out, out, out),
        in_specs=[in_vmem] * 2,
        out_specs=(in_hbm,) * 3,
        scratch_shapes=[pltpu.VMEM((3, X, Y, Z), f32), dma((3, chunks))],
        compiler_params=pltpu.CompilerParams(vmem_limit_bytes=16 * 1024 * 1024),
    )(rows, ends)


def solution(mesh):
    spec = P("gx", "gy", None)
    return jax.shard_map(
        functools.partial(per_device, mesh.shape["gx"], mesh.shape["gy"]),
        mesh=mesh,
        in_specs=(spec, spec, spec, spec, P("gx")),
        out_specs=(spec, spec, spec),
        check_vma=False,
    )
```
